32 devices in a mesh: dp: 8 (over z, y), mp: 4 (over x, core).
Axes of the slice: x: 2, y: 2, z: 4, core: 2. Of those that a mesh axis runs over, the one named last changes fastest.
Arguments:
- latents: bfloat16 [2, 16, 8192], P(None, None, ('dp', 'mp')), may hold values from -6 to 6
- noise: float32 [2, 16, 8192], P(None, None, ('dp', 'mp')), may hold values from -6 to 6
- timesteps: int32 [2, 8], P(None, 'dp'), may hold values from 0 to 999
- labels: int32 [2, 8], P(None, 'dp'), may hold values from 0 to 999
- grid: int32 [2, 2, 8], P(None, None, 'dp'), may hold values from 1 to 32, as said below
- flat_master: float32 [21430656], P(('dp', 'mp'))
- flat_moment: float32 [21430656], P(('dp', 'mp'))
- flat_second: float32 [21430656], P(('dp', 'mp'))
- tile_master: float32 [4, 96, 288, 288], P('mp', 'dp')
- tile_moment: float32 [4, 96, 288, 288], P('mp', 'dp'), may hold values from -9.536743e-06 to 9.536743e-06
- tile_left: float32 [4, 96, 288, 288], P('mp', 'dp')
- tile_right: float32 [4, 96, 288, 288], P('mp', 'dp')
- left_root: float32 [4, 96, 288, 288], P('mp', 'dp')
- right_root: float32 [4, 96, 288, 288], P('mp', 'dp')
Outputs:
- summed_loss: float32 [], replicated
- valid_count: float32 [], replicated
- grad_norm: float32 [], replicated
- flat_new_moment: float32 [21430656], P(('dp', 'mp'))
- flat_new_second: float32 [21430656], P(('dp', 'mp'))
- flat_new_master: float32 [21430656], P(('dp', 'mp'))
- tile_new_moment: float32 [4, 96, 288, 288], P('mp', 'dp')
- tile_new_left: float32 [4, 96, 288, 288], P('mp', 'dp')
- tile_new_right: float32 [4, 96, 288, 288], P('mp', 'dp')
- tile_new_master: float32 [4, 96, 288, 288], P('mp', 'dp')
The draws below stay inside these ranges and needn't reach their ends.
Inputs may be any that keep to these rules, and one draw needn't show every extreme that they name: `grid`: each latent has 1 to 32 patch rows and 1 to 32 patch columns; in every group one of its 2 latents has 32 rows and more than three quarters of 1024 valid slots.
All inputs are finite; a program needn't handle non-finite values.
Results may differ from the reference program's by a relative error of at most 0.0056.
Values may be sent and summed in bfloat16 or wider, within the bound.
A program may use at most 768 MiB of HBM per device.

```python
import math
import jax
import jax.numpy as jnp
import numpy as np
from jax import lax

D = 1152
HEADS = 16
HD = 72
FF = 4608
PATCH = 16
FREQ = 256
CLASSES = 1000
BLK = 288
LAYERS = 2
SIDE = 32
STEP_COUNT = 10
MB = 2
SEQ = 1024
QW = 288
FFM = 1152
TPR = 96
NFLAT = 21430656
NALL = 53281152
N_DP = 8
N_MP = 4


def gradient_size():
    return 0.005 * NALL ** (-0.5)


def flat_shapes_drawn():
    shapes = [(PATCH, D), (D,), (FREQ, D), (D,), (D, D), (D,), (CLASSES, D)]
    for layer in range(LAYERS):
        shapes = shapes + [(D, 6 * D), (6 * D,), (3 * D,), (D,), (FF,), (D,)]
    return shapes + [(D, 2 * D), (2 * D,), (D, PATCH)]


def statistic(key, offdiag, base, lowest, highest):
    diag = jnp.exp(jax.random.uniform(key, (N_MP, TPR, BLK), minval=math.log(lowest), maxval=math.log(highest)))
    sym = (offdiag + jnp.swapaxes(offdiag, 2, 3)) * 0.7071
    eye = jnp.eye(BLK, dtype=jnp.float32)
    return base * (diag[..., None] * eye + sym)


def draw_grid(key, part):
    key = jax.random.fold_in(key, 7)
    key_h, key_w, key_pick, key_full = jax.random.split(key, 4)
    groups = jnp.arange(N_DP)
    top = 2 + (SIDE - 2) * groups // max(N_DP - 1, 1)
    least = jnp.maximum(1, top * 3 // 4)
    height = jax.random.randint(key_h, (MB, N_DP), 0, 1 << 20) % (top - least + 1) + least
    width = jax.random.randint(key_w, (MB, N_DP), 0, 1 << 20) % (top - least + 1) + least
    pick = jax.random.randint(key_pick, (N_DP,), 0, MB)
    full_low = 3 * SIDE // 4 + 1 + (SIDE - 3 * SIDE // 4 - 1) * groups // max(N_DP - 1, 1)
    full_w = jax.random.randint(key_full, (N_DP,), 0, 1 << 20) % (SIDE - full_low + 1) + full_low
    chosen = jnp.arange(MB)[:, None] == pick[None, :]
    height = jnp.where(chosen, SIDE, height)
    width = jnp.where(chosen, full_w[None, :], width)
    return jnp.stack([height, width], axis=1).astype(jnp.int32)


def draw_flat_master(key, part):
    key = jax.random.fold_in(key, 3)
    scales = [PATCH ** (-0.5), 0.1, FREQ ** (-0.5), 0.1, D ** (-0.5), 0.1, D ** (-0.5)]
    for layer in range(LAYERS):
        scales = scales + [D ** (-0.5), 0.1, 0.1, 0.1, 0.1, 0.1]
    scales = scales + [D ** (-0.5), 0.1, D ** (-0.5)]
    scale = jnp.concatenate([jnp.full((math.prod(shape),), value, jnp.float32) for shape, value in zip(flat_shapes_drawn(), scales)])
    values = jax.random.normal(key, (NFLAT,))
    return values * scale


def draw_flat_moment(key, part):
    key = jax.random.fold_in(key, 23)
    size = 0.1 / 0.9 * gradient_size()
    values = jnp.clip(jax.random.normal(key, (NFLAT,)), -6.0, 6.0)
    return values * size


def draw_flat_second(key, part):
    key = jax.random.fold_in(key, 29)
    base = 0.001 / 0.999 * gradient_size() ** 2
    factor = jnp.exp(jax.random.uniform(key, (NFLAT,), minval=0.0, maxval=math.log(4.0)))
    return base * factor


def draw_tile_master(key, part):
    key = jax.random.fold_in(key, 5)
    per = TPR // LAYERS
    rows_d, rows_q, rows_f = (D // BLK, QW // BLK, FFM // BLK)
    first = rows_d * 3 * rows_q
    second = first + rows_q * rows_d
    third = second + rows_d * rows_f
    place = jnp.arange(TPR) % per
    scale = jnp.where(place < first, D ** (-0.5), jnp.where(place < second, 3.0 * D ** (-0.5), jnp.where(place < third, D ** (-0.5), FF ** (-0.5))))
    shape = (N_MP, TPR, BLK, BLK)
    values = jax.random.normal(key, shape)
    return values * scale[None, :, None, None]


def draw_tile_left(key, part):
    key = jax.random.fold_in(key, 11)
    key_diag, key_off = jax.random.split(key)
    shape = (N_MP, TPR, BLK, BLK)
    offdiag = 0.05 * jax.random.normal(key_off, shape)
    return statistic(key_diag, offdiag, 0.01 / 0.99 * BLK * gradient_size() ** 2, 1.0, 4.0)


def draw_tile_right(key, part):
    key = jax.random.fold_in(key, 13)
    key_diag, key_off = jax.random.split(key)
    shape = (N_MP, TPR, BLK, BLK)
    offdiag = 0.05 * jax.random.normal(key_off, shape)
    return statistic(key_diag, offdiag, 0.01 / 0.99 * BLK * gradient_size() ** 2, 1.0, 4.0)


def draw_left_root(key, part):
    key = jax.random.fold_in(key, 17)
    key_diag, key_off = jax.random.split(key)
    shape = (N_MP, TPR, BLK, BLK)
    offdiag = 0.05 * jax.random.normal(key_off, shape)
    return statistic(key_diag, offdiag, (0.01 / 0.99 * BLK * gradient_size() ** 2) ** (-0.25), 0.5, 2.0)


def draw_right_root(key, part):
    key = jax.random.fold_in(key, 19)
    key_diag, key_off = jax.random.split(key)
    shape = (N_MP, TPR, BLK, BLK)
    offdiag = 0.05 * jax.random.normal(key_off, shape)
    return statistic(key_diag, offdiag, (0.01 / 0.99 * BLK * gradient_size() ** 2) ** (-0.25), 0.5, 2.0)


def touch_ends(entries, stream_key, smallest, high):
    spot = [jax.random.randint(jax.random.fold_in(stream_key, axis), (), 0, length) for axis, length in enumerate(entries.shape)]
    main_axis = entries.shape.index(max(entries.shape))
    neighbour = spot[:main_axis] + [(spot[main_axis] + 1) % entries.shape[main_axis]] + spot[main_axis + 1:]
    return entries.at[tuple(spot)].set(smallest).at[tuple(neighbour)].set(high)


def level_of(rng, extent, cuts, low, high):
    def one(position, parts):
        heights = jax.random.uniform(jax.random.fold_in(jax.random.fold_in(rng, 6), position), (parts,), jnp.float32, low / len(cuts), high / len(cuts))
        return jnp.repeat(jnp.exp(heights), extent[position] // parts).reshape((-1,) + (1,) * (len(extent) - position - 1))

    loudness = one(*cuts[0])
    for cut in cuts[1:]:
        loudness = loudness * one(*cut)
    return loudness


def rank_table(count, skew):
    weights = [(1 << 20) // math.isqrt(standing ** skew) + 1 for standing in range(1, count + 1)]
    scale = 1 + sum(weights) // (1 << 30)
    return np.cumsum(np.array([max(1, weight // scale) for weight in weights]))


def skewed_ids(rng, extent, number_of, slope):
    table = rank_table(number_of, slope)
    ticket = jax.random.randint(jax.random.fold_in(rng, 1), extent, 0, int(table[number_of - 1]))
    standing = jnp.searchsorted(jnp.asarray(table, jnp.int32), ticket, side="right")
    return jax.random.permutation(jax.random.fold_in(rng, 2), number_of)[standing].astype(jnp.int32)


def normal_values(stream_key, shape, deviation, reach, cuts=(), held_as=jnp.bfloat16):
    result = jax.random.normal(stream_key, shape, jnp.float32) * deviation
    if len(cuts) > 0:
        result = level_of(stream_key, shape, cuts, -0.22, 0.18) * result
    return jnp.clip(result, min=-reach, max=reach).astype(held_as)


def setup_inputs(seed: int = 0) -> dict:
    key_list = jax.random.split(jax.random.key(seed), 15)
    latents = normal_values(key_list[0], (MB, PATCH, N_DP * SEQ), 1.0, 6.0, ((2, 32),))
    noise = normal_values(key_list[1], (MB, PATCH, N_DP * SEQ), 1.0, 6.0, ((2, 32),), jnp.float32)
    timesteps = touch_ends(jax.random.randint(key_list[2], (MB, N_DP), 0, 1000), jax.random.fold_in(key_list[2], 1), 0, 999).astype(jnp.int32)
    labels = touch_ends(skewed_ids(key_list[3], (MB, N_DP), CLASSES, 2), jax.random.fold_in(key_list[3], 3), 0, CLASSES - 1).astype(jnp.int32)
    grid = draw_grid(jax.random.fold_in(key_list[14], 71), 0)
    flat_master = draw_flat_master(jax.random.fold_in(key_list[14], 71), 0)
    flat_moment = draw_flat_moment(jax.random.fold_in(key_list[14], 71), 0)
    flat_second = draw_flat_second(jax.random.fold_in(key_list[14], 71), 0)
    tile_master = draw_tile_master(jax.random.fold_in(key_list[14], 71), 0)
    tile_moment = normal_values(key_list[9], (N_MP, TPR, BLK, BLK), (0.005 * NALL ** -0.5), 9.5367431640625e-06, ((0, 4), (1, 8)), jnp.float32)
    tile_left = draw_tile_left(jax.random.fold_in(key_list[14], 71), 0)
    tile_right = draw_tile_right(jax.random.fold_in(key_list[14], 71), 0)
    left_root = draw_left_root(jax.random.fold_in(key_list[14], 71), 0)
    right_root = draw_right_root(jax.random.fold_in(key_list[14], 71), 0)
    return dict(latents=latents, noise=noise, timesteps=timesteps, labels=labels, grid=grid, flat_master=flat_master, flat_moment=flat_moment, flat_second=flat_second, tile_master=tile_master, tile_moment=tile_moment, tile_left=tile_left, tile_right=tile_right, left_root=left_root, right_root=right_root)


@jax.custom_vjp
def low(v):
    return lax.optimization_barrier(v.astype(jnp.bfloat16)).astype(jnp.float32)

@jax.custom_vjp
def low_back(v):
    return v

def low_keep(v):
    return (low(v), None)

def low_pass(kept, grad):
    return (grad,)

def back_keep(v):
    return (v, None)

def back_low(kept, grad):
    return (low(grad),)
low.defvjp(low_keep, low_pass)
low_back.defvjp(back_keep, back_low)
HIGH = lax.Precision.HIGHEST
NORM_EPS = 1e-06
CLIP_AT = 0.005
ADAM_ONE = 0.9
ADAM_TWO = 0.999
ADAM_EPS = 1e-08
ADAM_RATE = 0.02
ADAM_DECAY = 0.01
SHAMPOO_ONE = 0.9
SHAMPOO_TWO = 0.99
SHAMPOO_RATE = 0.01
SHAMPOO_DECAY = 0.01

def flat_shapes():
    shapes = [(PATCH, D), (D,), (FREQ, D), (D,), (D, D), (D,), (CLASSES, D)]
    for layer in range(LAYERS):
        shapes = shapes + [(D, 6 * D), (6 * D,), (3 * D,), (D,), (FF,), (D,)]
    return shapes + [(D, 2 * D), (2 * D,), (D, PATCH)]

def unflat(flat):
    pieces = []
    start = 0
    for shape in flat_shapes():
        amount = math.prod(shape)
        pieces.append(lax.slice_in_dim(flat, start, start + amount).reshape(shape))
        start = start + amount
    return pieces

def untile(tiles, height, breadth):
    return tiles.reshape(height // BLK, breadth // BLK, BLK, BLK).transpose(0, 2, 1, 3).reshape(height, breadth)

def time_freq(step):
    half = FREQ // 2
    freqs = jnp.exp(-math.log(10000.0) * jnp.arange(half).astype(jnp.float32) / half)
    angles = step.astype(jnp.float32) * freqs
    return jnp.concatenate([jnp.cos(angles), jnp.sin(angles)])

def place_embed(slots, width):
    quarter = D // 4
    omega = jnp.power(10000.0, -jnp.arange(quarter).astype(jnp.float32) / quarter)
    row_angle = (slots // width).astype(jnp.float32)[:, None] * omega
    col_angle = (slots % width).astype(jnp.float32)[:, None] * omega
    return jnp.concatenate([jnp.sin(row_angle), jnp.cos(row_angle), jnp.sin(col_angle), jnp.cos(col_angle)], axis=1)

def normalize(state):
    centered = state - lax.optimization_barrier(jnp.mean(state, axis=-1, keepdims=True))
    spread = lax.optimization_barrier(jnp.mean(centered * centered, axis=-1, keepdims=True))
    return centered * lax.rsqrt(spread + NORM_EPS)

def modulate(state, shift, scale):
    return normalize(state) * (1.0 + scale) + shift

def condition(time_w1, time_b1, time_w2, time_b2, table, step, label):
    hidden = jax.nn.silu(jnp.dot(time_freq(step), time_w1, precision=HIGH) + time_b1)
    embed = jnp.dot(hidden, time_w2, precision=HIGH) + time_b2
    return embed + lax.dynamic_index_in_dim(table, label, 0, keepdims=False)

def full_mats(tiles, layer):
    per = TPR // LAYERS
    rows_d, rows_q, rows_f = (D // BLK, QW // BLK, FFM // BLK)
    first = rows_d * 3 * rows_q
    second = first + rows_q * rows_d
    third = second + rows_d * rows_f
    mixers, projs, ups, downs = ([], [], [], [])
    for rank in range(N_MP):
        part = tiles[rank, layer * per:(layer + 1) * per]
        mixers.append(untile(part[:first], D, 3 * QW).reshape(D, 3, QW))
        projs.append(untile(part[first:second], QW, D))
        ups.append(untile(part[second:third], D, FFM))
        downs.append(untile(part[third:], FFM, D))
    mixer = jnp.stack(mixers, axis=2).reshape(D, 3 * D)
    return (mixer, jnp.concatenate(projs, 0), jnp.concatenate(ups, 1), jnp.concatenate(downs, 0))

def attend_block(block_query, keys, values, keymask):
    raw = jnp.einsum('qhd,khd->hqk', block_query, keys, precision=HIGH) * HD ** (-0.5)
    scores = jnp.where(keymask[None, None, :], low_back(raw), -1e+30)
    probs = low(jax.nn.softmax(scores, axis=-1))
    return jnp.einsum('hqk,khd->qhd', probs, values, precision=HIGH)

def sequence_loss(tiles, flat, patches, target, step, label, height, width, count):
    pieces = unflat(flat)
    patch_w, patch_b, time_w1, time_b1, time_w2, time_b2, table = pieces[:7]
    cond = condition(time_w1, time_b1, time_w2, time_b2, table, step, label)
    cond_s = low(jax.nn.silu(cond))
    slots = jnp.arange(SEQ)
    valid = slots < height * width
    state = jnp.dot(patches.T, patch_w, precision=HIGH) + patch_b + place_embed(slots, width)
    block = 512 if SEQ % 512 == 0 else SEQ
    for layer in range(LAYERS):
        ada_w, ada_b, qkv_b, proj_b, up_b, down_b = pieces[7 + 6 * layer:13 + 6 * layer]
        mixer, proj, up_w, down_w = full_mats(tiles, layer)
        modulation = jnp.dot(cond_s, ada_w, precision=HIGH) + ada_b
        shift_a, scale_a, gate_a, shift_b, scale_b, gate_b = jnp.split(modulation, 6)
        normed_a = low(modulate(state, shift_a, scale_a))
        mixed = low(low_back(jnp.dot(normed_a, mixer, precision=HIGH) + qkv_b))
        query, keys, values = [mixed[:, part * D:(part + 1) * D].reshape(SEQ, HEADS, HD) for part in range(3)]

        def one_block(block_query):
            return attend_block(block_query, keys, values, valid)
        attended = lax.map(jax.checkpoint(one_block), query.reshape(SEQ // block, block, HEADS, HD))
        attended = low(low_back(attended.reshape(SEQ, D)))
        attn = low_back(jnp.dot(attended, proj, precision=HIGH)) + proj_b
        middle = state + gate_a * attn
        normed_b = low(modulate(middle, shift_b, scale_b))
        pre_act = low_back(jnp.dot(normed_b, up_w, precision=HIGH) + up_b)
        active = low(jax.nn.gelu(pre_act, approximate=True))
        mlp = low_back(jnp.dot(active, down_w, precision=HIGH)) + down_b
        state = middle + gate_b * mlp
    final_w, final_b, head_w = pieces[-3:]
    final_mod = jnp.dot(cond_s, final_w, precision=HIGH) + final_b
    shift_f, scale_f = jnp.split(final_mod, 2)
    normed_f = low(modulate(state, shift_f, scale_f))
    predicted = low_back(jnp.dot(normed_f, head_w, precision=HIGH))
    error = predicted - target.T
    summed = jnp.sum(jnp.where(valid[:, None], error * error, 0.0))
    return (summed / (PATCH * count), summed)

def adamw(grad, moment, second, master):
    new_moment = ADAM_ONE * moment + (1.0 - ADAM_ONE) * grad
    new_second = ADAM_TWO * second + (1.0 - ADAM_TWO) * grad * grad
    fixed_moment = new_moment / (1.0 - ADAM_ONE ** STEP_COUNT)
    fixed_second = new_second / (1.0 - ADAM_TWO ** STEP_COUNT)
    new_master = master - ADAM_RATE * (fixed_moment / (jnp.sqrt(fixed_second) + ADAM_EPS) + ADAM_DECAY * master)
    return (new_moment, new_second, new_master)

def shampoo(grad, moment, left, right, left_inv, right_inv, master):
    new_left = SHAMPOO_TWO * left + (1.0 - SHAMPOO_TWO) * jnp.einsum('tij,tkj->tik', grad, grad, precision=HIGH)
    new_right = SHAMPOO_TWO * right + (1.0 - SHAMPOO_TWO) * jnp.einsum('tji,tjk->tik', grad, grad, precision=HIGH)
    new_moment = SHAMPOO_ONE * moment + (1.0 - SHAMPOO_ONE) * grad
    halfway = jnp.einsum('tij,tjk->tik', left_inv, new_moment, precision=HIGH)
    direction = jnp.einsum('tij,tjk->tik', halfway, right_inv, precision=HIGH)
    new_master = master - SHAMPOO_RATE * (direction + SHAMPOO_DECAY * master)
    return (new_moment, new_left, new_right, new_master)

def reference(latents, noise, timesteps, labels, grid, flat_master, flat_moment, flat_second, tile_master, tile_moment, tile_left, tile_right, left_root, right_root):
    tiles = tile_master.astype(jnp.bfloat16).astype(jnp.float32)
    flat = flat_master.astype(jnp.bfloat16).astype(jnp.float32)
    count = jnp.sum((grid[:, 0, :] * grid[:, 1, :]).astype(jnp.float32))

    def one_sequence(carry, index):
        grad_tiles, grad_flat, total = carry
        batch = index // N_DP
        group = index % N_DP
        patches = lax.dynamic_slice_in_dim(lax.dynamic_index_in_dim(latents, batch, 0, keepdims=False), group * SEQ, SEQ, 1).astype(jnp.float32)
        target = lax.dynamic_slice_in_dim(lax.dynamic_index_in_dim(noise, batch, 0, keepdims=False), group * SEQ, SEQ, 1)
        step = timesteps[batch, group]
        label = labels[batch, group]
        height = grid[batch, 0, group]
        width = grid[batch, 1, group]

        def loss_of(tile_arg, flat_arg):
            return sequence_loss(tile_arg, flat_arg, patches, target, step, label, height, width, count)
        loss, pull, summed = jax.vjp(loss_of, tiles, flat, has_aux=True)
        grad_t, grad_f = pull(jnp.ones_like(loss))
        return ((grad_tiles + grad_t, grad_flat + grad_f, total + summed), None)
    start = (jnp.zeros(tiles.shape, jnp.float32), jnp.zeros(flat.shape, jnp.float32), jnp.zeros((), jnp.float32))
    (grad_tiles, grad_flat, total), unused = lax.scan(one_sequence, start, jnp.arange(MB * N_DP).astype(jnp.int32))
    norm = jnp.sqrt(jnp.sum(grad_flat * grad_flat) + jnp.sum(grad_tiles * grad_tiles))
    factor = jnp.minimum(1.0, CLIP_AT / (norm + 1e-06))
    new_moment, new_second, new_flat = adamw(grad_flat * factor, flat_moment, flat_second, flat_master)
    shape = tile_master.shape

    def blocks(array):
        return array.reshape(-1, BLK, BLK)
    tile_mom, new_left, new_right, new_tiles = shampoo(blocks(grad_tiles * factor), blocks(tile_moment), blocks(tile_left), blocks(tile_right), blocks(left_root), blocks(right_root), blocks(tile_master))
    return (total, count, norm, new_moment, new_second, new_flat, tile_mom.reshape(shape), new_left.reshape(shape), new_right.reshape(shape), new_tiles.reshape(shape))
```

```python
import math

import jax
import jax.numpy as jnp
from jax import lax
from jax.sharding import Mesh
from jax.sharding import PartitionSpec as P

D = 1152
HD = 72
FF = 4608
PATCH = 16
FREQ = 256
CLASSES = 1000
BLK = 288
LAYERS = 2
STEP_COUNT = 10
MB = 2
LANE = 128
STRIP = 3 * BLK


HIGH = lax.Precision.HIGHEST
NORM_EPS = 1e-06
CLIP_AT = 0.005
ADAM_ONE = 0.9
ADAM_TWO = 0.999
ADAM_EPS = 1e-08
ADAM_RATE = 0.02
ADAM_DECAY = 0.01
SHAMPOO_ONE = 0.9
SHAMPOO_TWO = 0.99
SHAMPOO_RATE = 0.01
SHAMPOO_DECAY = 0.01

F32 = jnp.float32
BF16 = jnp.bfloat16
SWAP = [(0, 1), (1, 0)]

ROW_D = D // LANE
ROW_STEM = (PATCH + 1) * ROW_D
BASE_W1 = ROW_STEM
BASE_B1 = BASE_W1 + FREQ * ROW_D
BASE_W2 = BASE_B1 + ROW_D
BASE_B2 = BASE_W2 + D * ROW_D
BASE_TABLE = BASE_B2 + ROW_D
BASE_LAYER = BASE_TABLE + CLASSES * ROW_D
ROW_ADA = 6 * ROW_D
ROW_BIAS = (6 + 3 + 1 + 4 + 1) * ROW_D
LAYER_ROWS = D * ROW_ADA + ROW_BIAS
BASE_FINAL = BASE_LAYER + LAYERS * LAYER_ROWS
ROW_FINAL = 2 * ROW_D
BASE_TAIL = BASE_FINAL + D * ROW_FINAL
ROW_TAIL = ROW_FINAL + PATCH * ROW_D
FRONT = 56


def time_freq(step):
    half = FREQ // 2
    freqs = jnp.exp(-math.log(10000.0) * jnp.arange(half).astype(F32) / half)
    angles = step.astype(F32) * freqs
    return jnp.concatenate([jnp.cos(angles), jnp.sin(angles)])


def place_embed(slots, width):
    quarter = D // 4
    omega = jnp.power(10000.0, -jnp.arange(quarter).astype(F32) / quarter)
    row_angle = (slots // width).astype(F32)[:, None] * omega
    col_angle = (slots % width).astype(F32)[:, None] * omega
    return jnp.concatenate(
        [jnp.sin(row_angle), jnp.cos(row_angle), jnp.sin(col_angle), jnp.cos(col_angle)], axis=1
    )


def normalize(state):
    centered = state - jnp.mean(state, axis=-1, keepdims=True)
    spread = jnp.mean(centered * centered, axis=-1, keepdims=True)
    return centered * lax.rsqrt(spread + NORM_EPS)


def modulate(state, shift, scale):
    return normalize(state) * (1.0 + scale) + shift


def gelu_tanh(value):
    return jax.nn.gelu(value, approximate=True)


def contract_rows(left, right):
    return lax.dot_general(left, right, (((0,), (0,)), ((), ())), preferred_element_type=F32)


def contract_cols(left, right):
    return lax.dot_general(left, right, (((1,), (1,)), ((), ())), preferred_element_type=F32)


def bits_of(axis):
    size = lax.axis_size(axis)
    return [1 << k for k in range(size.bit_length() - 1)]


def swap_by(value, axis, bit):
    size = lax.axis_size(axis)
    return lax.ppermute(value, axis, [(i, i ^ bit) for i in range(size)])


def all_sum(value, axes=("c", "x", "y", "z")):
    for axis in axes:
        for bit in bits_of(axis):
            value = value + swap_by(value, axis, bit)
    return value


def gather_rows(value, axes):
    for axis in axes:
        for bit in bits_of(axis):
            other = swap_by(value, axis, bit)
            low = (lax.axis_index(axis) & bit) == 0
            value = jnp.where(
                low, jnp.concatenate([value, other]), jnp.concatenate([other, value])
            )
    return value


def scatter_rows(value, axes):
    for axis in axes:
        for bit in reversed(bits_of(axis)):
            halves = value.reshape((2, value.shape[0] // 2) + value.shape[1:])
            side = jnp.where((lax.axis_index(axis) & bit) == 0, 0, 1)
            send = lax.dynamic_index_in_dim(halves, 1 - side, 0, keepdims=False)
            keep = lax.dynamic_index_in_dim(halves, side, 0, keepdims=False)
            value = keep + swap_by(send, axis, bit)
    return value


def own_sequence(values):
    x = lax.axis_index("x")
    send = lax.dynamic_index_in_dim(values, 1 - x, 0, keepdims=False)
    keep = lax.dynamic_index_in_dim(values, x, 0, keepdims=False)
    other = lax.ppermute(send, "x", SWAP)
    pair = jnp.where(x == 0, jnp.stack([keep, other]), jnp.stack([other, keep]))
    more = lax.ppermute(pair, "c", SWAP)
    both = jnp.where(
        lax.axis_index("c") == 0, jnp.stack([pair, more], 1), jnp.stack([more, pair], 1)
    )
    return both.transpose(2, 0, 1, 3).reshape(values.shape[1], -1)


def strips_of(tiles, is_mixer):
    count = tiles.shape[0] // 12
    plain = (
        tiles.reshape(count, 3, 4, BLK, BLK).transpose(0, 1, 3, 2, 4).reshape(count, STRIP, D)
    )
    turned = (
        tiles.reshape(count, 4, 3, BLK, BLK).transpose(0, 2, 4, 1, 3).reshape(count, STRIP, D)
    )
    return jnp.where(is_mixer, turned, plain)


def tiles_of(strips, is_mixer):
    count = strips.shape[0]
    plain = (
        strips.reshape(count, 3, BLK, 4, BLK).transpose(0, 1, 3, 2, 4).reshape(-1, BLK, BLK)
    )
    turned = (
        strips.reshape(count, 3, BLK, 4, BLK).transpose(0, 3, 1, 4, 2).reshape(-1, BLK, BLK)
    )
    return jnp.where(is_mixer, turned, plain)


def select_y(own, other):
    first = lax.axis_index("y") == 0
    return jnp.where(first, own, other), jnp.where(first, other, own)


HALF = STRIP // 2


def gather_strips(strip):
    z = lax.axis_index("z")
    halves = []
    for part in (strip[:HALF], strip[HALF:]):
        right, left = [part], [part]
        for hop in range(3):
            right.append(lax.ppermute(right[-1], "z", [(i, i + 1) for i in range(hop, 3)]))
            left.append(lax.ppermute(left[-1], "z", [(i + 1, i) for i in range(3 - hop)]))
        halves.append((right, left))
    planes = []
    for plane in range(4):
        columns = []
        for right, left in halves:
            column = right[0]
            for place in range(4):
                if place > plane:
                    column = jnp.where(z == place, right[place - plane], column)
                elif place < plane:
                    column = jnp.where(z == place, left[plane - place], column)
            columns.append(column)
        upper, lower = columns
        upper_x = lax.ppermute(upper, "x", SWAP)
        upper_y = lax.ppermute(jnp.stack([upper, upper_x]), "y", SWAP)
        lower_y = lax.ppermute(lower, "y", SWAP)
        lower_x = lax.ppermute(jnp.stack([lower, lower_y]), "x", SWAP)
        own_y = [
            jnp.concatenate([upper, lower]),
            jnp.concatenate([upper_x, lower_x[0]]),
        ]
        other_y = [
            jnp.concatenate([upper_y[0], lower_y]),
            jnp.concatenate([upper_y[1], lower_x[1]]),
        ]
        planes.append([select_y(own_y[i], other_y[i]) for i in range(2)])
    return planes


def gather_any(tiles):
    whole = lax.all_gather(tiles, ("z", "y", "x"), axis=0, tiled=False)
    x = lax.axis_index("x")
    whole = whole.reshape((-1, 2) + tiles.shape)
    groups = []
    for place in (x, 1 - x):
        blocks = lax.dynamic_index_in_dim(whole, place, 1, keepdims=False)
        blocks = blocks.reshape(-1, BLK, BLK)
        groups.append(strips_of(blocks, (jnp.arange(8) % 4 == 0)[:, None, None]))
    return [
        [(groups[i][2 * plane], groups[i][2 * plane + 1]) for i in range(2)] for plane in range(4)
    ]


def add_low(left, right):
    return (left.astype(F32) + right.astype(F32)).astype(BF16)


def reduce_plane(grads):
    y = lax.axis_index("y")

    def pick(pair, own):
        first = (y == 0) if own else (y == 1)
        return jnp.where(first, pair[0], pair[1])

    own_x = [part[:HALF] for part in grads[0]]
    send_x = jnp.stack([part[:HALF] for part in grads[1]])
    got = lax.ppermute(send_x, "x", SWAP)
    upper = [add_low(own_x[i], got[i]) for i in range(2)]
    got = lax.ppermute(pick(upper, False), "y", SWAP)
    upper = add_low(pick(upper, True), got)
    lows = [[part[HALF:] for part in group] for group in grads]
    got = lax.ppermute(jnp.stack([pick(group, False) for group in lows]), "y", SWAP)
    lower = [add_low(pick(lows[i], True), got[i]) for i in range(2)]
    got = lax.ppermute(lower[1], "x", SWAP)
    lower = add_low(lower[0], got)
    return [upper, lower]


def reduce_line(part, plane):
    rights, lefts = plane, 3 - plane
    hops = max(rights, lefts)
    for hop in range(hops):
        pairs = []
        if hop < rights:
            pairs.append((hop, hop + 1))
        if hop < lefts:
            pairs.append((3 - hop, 2 - hop))
        if len(pairs) == 2 and pairs[0][1] == pairs[1][1]:
            one = lax.ppermute(part, "z", [pairs[0]])
            two = lax.ppermute(part, "z", [pairs[1]])
            part = add_low(part, one.astype(F32) + two.astype(F32))
        else:
            part = add_low(part, lax.ppermute(part, "z", pairs))
    return part


def reduce_any(planes, count):
    x = lax.axis_index("x")
    groups = []
    for place in range(2):
        chosen = [
            jnp.where(x == place, planes[plane][0][y], planes[plane][1][y])
            for plane in range(4)
            for y in range(2)
        ]
        blocks = tiles_of(jnp.stack(chosen), jnp.zeros((), bool)).reshape(8, 12, BLK, BLK)
        turned = tiles_of(jnp.stack(chosen), jnp.ones((), bool)).reshape(8, 12, BLK, BLK)
        mixer = (jnp.arange(8) % 4 == 0)[:, None, None, None]
        groups.append(jnp.where(mixer, turned, blocks).reshape(-1, count, BLK, BLK))
    whole = jnp.stack(groups, axis=1).reshape(-1, BLK, BLK)
    return lax.psum_scatter(whole, ("z", "y", "x"), scatter_dimension=0, tiled=True)


class Flat:
    def __init__(self, length):
        size = lax.axis_size("z") * lax.axis_size("y") * lax.axis_size("x") * lax.axis_size("c")
        del size
        index = lax.axis_index("z")
        for axis in ("y", "x", "c"):
            index = index * lax.axis_size(axis) + lax.axis_index(axis)
        start = index * length
        self.length = length
        self.first = start // LANE
        self.skew = start % LANE
        self.rows = -(-(length + LANE - 1) // LANE)
        self.back = self.rows + 2 * ROW_ADA
        self.total = -(-(FRONT + self.rows + self.back) // 8) * 8

    def align(self, shard):
        empty = jnp.zeros((self.total * LANE,), shard.dtype)
        return lax.dynamic_update_slice(empty, shard, (FRONT * LANE + self.skew,)).reshape(
            self.total, LANE
        )

    def unalign(self, rows):
        return lax.dynamic_slice(
            rows.reshape(-1), (FRONT * LANE + self.skew,), (self.length,)
        )

    def place(self, base, width, height):
        count = min(height, self.rows // width + 2)
        skip = jnp.clip((self.first - base) // width, 0, height)
        at = jnp.minimum(base + skip * width - self.first, self.rows) + FRONT
        return count, skip, at

    def part(self, rows, base, width, height):
        count, skip, at = self.place(base, width, height)
        piece = lax.dynamic_slice(rows, (at, 0), (count * width, LANE))
        return piece.reshape(count, width * LANE), count, skip

    def product(self, rows, factor, base, width, precision=None):
        height = factor.shape[1]
        piece, count, skip = self.part(rows, base, width, height)
        padded = jnp.pad(factor, ((0, 0), (0, count)))
        near = lax.dynamic_slice(padded, (0, skip), (factor.shape[0], count))
        return jnp.dot(near, piece, precision=precision, preferred_element_type=F32)

    def back_product(self, rows, grad, base, width, height):
        piece, count, skip = self.part(rows, base, width, height)
        piece = piece.astype(F32)
        near = lax.dot_general(
            grad, piece, (((1,), (1,)), ((), ())), precision=HIGH, preferred_element_type=F32
        )
        empty = jnp.zeros((grad.shape[0], height + count), F32)
        return lax.dynamic_update_slice(empty, near, (0, skip))[:, :height]

    def take(self, rows, base, height):
        count, skip, at = self.place(base, 1, height)
        count = height
        piece = lax.dynamic_slice(rows, (at, 0), (count, LANE))
        keep = jnp.arange(count) < height - skip
        piece = jnp.where(keep[:, None], piece, 0)
        empty = jnp.zeros((2 * height, LANE), rows.dtype)
        return lax.dynamic_update_slice(empty, piece, (skip, 0))[:height]

    def put_outer(self, rows, left, right, base, width):
        height = left.shape[1]
        count, skip, at = self.place(base, width, height)
        padded = jnp.pad(left, ((0, 0), (0, count)))
        near = lax.dynamic_slice(padded, (0, skip), (left.shape[0], count))
        piece = lax.dot_general(
            near, right, (((0,), (0,)), ((), ())), precision=HIGH, preferred_element_type=F32
        )
        return lax.dynamic_update_slice(rows, piece.reshape(count * width, LANE), (at, 0))

    def put_rows(self, rows, vector, base):
        height = vector.shape[0]
        unused, skip, at = self.place(base, 1, height)
        padded = jnp.pad(vector, ((0, height), (0, 0)))
        near = lax.dynamic_slice(padded, (skip, 0), (height, LANE))
        return lax.dynamic_update_slice(rows, near, (at, 0))


def split_heads(mixed):
    rows = mixed.shape[0]
    heads = mixed.shape[1] // (3 * HD)
    shaped = mixed.reshape(rows, 3, heads, HD)
    return (shaped[:, 0], shaped[:, 1], shaped[:, 2])


def query_block(rows):
    return 512 if rows % 512 == 0 else rows


def attend_forward(mixed, keymask):
    query, keys, values = split_heads(mixed)
    rows, heads = (query.shape[0], query.shape[1])
    block = query_block(rows)
    scale = HD ** (-0.5)

    def one_block(block_query):
        raw = (
            jnp.einsum("qhd,khd->hqk", block_query, keys, preferred_element_type=F32)
            * scale
        )
        scores = jnp.where(keymask[None, None, :], raw, -1e30)
        top = jnp.max(scores, axis=-1, keepdims=True)
        expo = jnp.exp(scores - top)
        total = jnp.sum(expo, axis=-1, keepdims=True)
        probs = (expo / total).astype(BF16)
        out = jnp.einsum("hqk,khd->qhd", probs, values, preferred_element_type=F32)
        return (out, (top + jnp.log(total))[..., 0])

    outs, log_total = lax.map(one_block, query.reshape(rows // block, block, heads, HD))
    return (outs.reshape(rows, heads * HD).astype(BF16), log_total)


def attend_backward(mixed, keymask, log_total, attended, grad_out):
    query, keys, values = split_heads(mixed)
    rows, heads = (query.shape[0], query.shape[1])
    block = query_block(rows)
    scale = HD ** (-0.5)

    def one_block(carry, inputs):
        grad_keys, grad_values = carry
        block_query, block_total, block_grad = inputs
        raw = (
            jnp.einsum("qhd,khd->hqk", block_query, keys, preferred_element_type=F32)
            * scale
        )
        scores = jnp.where(keymask[None, None, :], raw, -1e30)
        probs = jnp.exp(scores - block_total[..., None])
        grad_probs = jnp.einsum("qhd,khd->hqk", block_grad, values, preferred_element_type=F32)
        delta = jnp.sum(grad_probs * probs, axis=-1, keepdims=True)
        grad_scores = (probs * (grad_probs - delta)).astype(BF16)
        grad_query = (
            jnp.einsum("hqk,khd->qhd", grad_scores, keys, preferred_element_type=F32)
            * scale
        )
        grad_keys = (
            grad_keys
            + jnp.einsum("hqk,qhd->khd", grad_scores, block_query, preferred_element_type=F32)
            * scale
        )
        grad_values = grad_values + jnp.einsum(
            "hqk,qhd->khd", probs.astype(BF16), block_grad, preferred_element_type=F32
        )
        return ((grad_keys, grad_values), grad_query)

    empty = jnp.zeros(keys.shape, F32)
    shaped = (
        query.reshape(rows // block, block, heads, HD),
        log_total,
        grad_out.reshape(rows // block, block, heads, HD),
    )
    (grad_keys, grad_values), grad_query = lax.scan(one_block, (empty, empty), shaped)
    return (
        jnp.stack([grad_query.reshape(rows, heads, HD), grad_keys, grad_values], axis=1)
        .reshape(mixed.shape)
        .astype(BF16)
    )


def join_cores(partial):
    low = partial.astype(BF16)
    return low.astype(F32) + lax.ppermute(low, "c", SWAP).astype(F32)


def rank_columns(vector, groups, rank, ranks):
    return lax.dynamic_index_in_dim(
        vector.reshape(groups, ranks, -1), rank, 1, keepdims=False
    ).reshape(-1)


def spread_columns(grads, groups, ranks_here, ranks):
    total = 0.0
    for grad, rank in zip(grads, ranks_here):
        width = grad.shape[0] // groups
        select = (jnp.arange(ranks) == rank).astype(F32)
        total = total + (grad.reshape(groups, 1, width) * select[None, :, None]).reshape(-1)
    return total


def layer_forward(state, modulation, biases, mats, keymask, ranks_here, ranks):
    qkv_b, proj_b, up_b, down_b = biases
    shift_a, scale_a, gate_a, shift_b, scale_b, gate_b = jnp.split(modulation, 6)
    normed_a = modulate(state, shift_a, scale_a).astype(BF16)
    mixed, log_total, attended = ([], [], [])
    partial = 0.0
    for mat, rank in zip(mats, ranks_here):
        bias = rank_columns(qkv_b, 3, rank, ranks)
        one = (contract_cols(normed_a, mat[0]) + bias).astype(BF16)
        out, total = attend_forward(one, keymask)
        mixed.append(one)
        log_total.append(total)
        attended.append(out)
        partial = partial + jnp.dot(out, mat[1], preferred_element_type=F32)
    attn = join_cores(partial) + proj_b
    middle = state + gate_a * attn
    normed_b = modulate(middle, shift_b, scale_b).astype(BF16)
    pre_act, active = ([], [])
    partial = 0.0
    for mat, rank in zip(mats, ranks_here):
        bias = rank_columns(up_b, 1, rank, ranks)
        pre = jnp.dot(normed_b, mat[2], preferred_element_type=F32) + bias
        act = gelu_tanh(pre).astype(BF16)
        pre_act.append(pre)
        active.append(act)
        partial = partial + jnp.dot(act, mat[3], preferred_element_type=F32)
    mlp = join_cores(partial) + down_b
    kept = (state, normed_a, mixed, log_total, attended, attn, middle, normed_b, pre_act, active, mlp)
    return (middle + gate_b * mlp, kept)


def layer_backward(grad_out, modulation, mats, kept, keymask, ranks_here, ranks):
    state, normed_a, mixed, log_total, attended, attn, middle, normed_b, pre_act, active, mlp = kept
    shift_a, scale_a, gate_a, shift_b, scale_b, gate_b = jnp.split(modulation, 6)
    grad_gate_b = jnp.sum(grad_out * mlp, axis=0)
    grad_mlp = gate_b * grad_out
    grad_down_b = jnp.sum(grad_mlp, axis=0)
    grad_mlp = grad_mlp.astype(BF16)
    grad_up, grad_down, grad_up_b = ([], [], [])
    partial = 0.0
    for mat, pre, act in zip(mats, pre_act, active):
        grad_down.append(contract_rows(act, grad_mlp).astype(BF16))
        grad_act = contract_cols(grad_mlp, mat[3])
        unused, gelu_pull = jax.vjp(gelu_tanh, pre)
        grad_pre = gelu_pull(grad_act)[0].astype(BF16)
        grad_up_b.append(jnp.sum(grad_pre.astype(F32), axis=0))
        grad_up.append(contract_rows(normed_b, grad_pre).astype(BF16))
        partial = partial + contract_cols(grad_pre, mat[2])
    unused, pull_b = jax.vjp(modulate, middle, shift_b, scale_b)
    grad_inner, grad_shift_b, grad_scale_b = pull_b(join_cores(partial))
    grad_middle = grad_out + grad_inner
    grad_gate_a = jnp.sum(grad_middle * attn, axis=0)
    grad_attn = gate_a * grad_middle
    grad_proj_b = jnp.sum(grad_attn, axis=0)
    grad_attn = grad_attn.astype(BF16)
    grad_proj, grad_mixer, grad_qkv_b = ([], [], [])
    partial = 0.0
    for mat, one, total, out in zip(mats, mixed, log_total, attended):
        grad_proj.append(contract_rows(out, grad_attn).astype(BF16))
        grad_attended = contract_cols(grad_attn, mat[1]).astype(BF16)
        grad_mixed = attend_backward(one, keymask, total, out, grad_attended)
        grad_qkv_b.append(jnp.sum(grad_mixed.astype(F32), axis=0))
        grad_mixer.append(contract_rows(grad_mixed, normed_a).astype(BF16))
        partial = partial + jnp.dot(grad_mixed, mat[0], preferred_element_type=F32)
    unused, pull_a = jax.vjp(modulate, state, shift_a, scale_a)
    grad_state, grad_shift_a, grad_scale_a = pull_a(join_cores(partial))
    grad_mod = jnp.concatenate(
        [grad_shift_a, grad_scale_a, grad_gate_a, grad_shift_b, grad_scale_b, grad_gate_b]
    )
    once = jnp.where(lax.axis_index("c") == 0, 1.0, 0.0)
    grad_bias = jnp.concatenate(
        [
            spread_columns(grad_qkv_b, 3, ranks_here, ranks),
            grad_proj_b * once,
            spread_columns(grad_up_b, 1, ranks_here, ranks),
            grad_down_b * once,
        ]
    )
    split = 2 * BLK
    upper = [
        (grad_mixer[i], jnp.concatenate([grad_proj[i], grad_up[i][:split]])) for i in range(2)
    ]
    lower = [
        (jnp.concatenate([grad_up[i][split:], grad_down[i][:BLK]]), grad_down[i][BLK:])
        for i in range(2)
    ]
    return (grad_middle + grad_state, grad_mod, grad_bias, [upper, lower])


def adamw(grad, moment, second, master):
    new_moment = ADAM_ONE * moment + (1.0 - ADAM_ONE) * grad
    new_second = ADAM_TWO * second + (1.0 - ADAM_TWO) * grad * grad
    fixed_moment = new_moment / (1.0 - ADAM_ONE**STEP_COUNT)
    fixed_second = new_second / (1.0 - ADAM_TWO**STEP_COUNT)
    new_master = master - ADAM_RATE * (
        fixed_moment / (jnp.sqrt(fixed_second) + ADAM_EPS) + ADAM_DECAY * master
    )
    return (new_moment, new_second, new_master)


def shampoo(grad, moment, left, right, left_inv, right_inv, master):
    new_left = SHAMPOO_TWO * left + (1.0 - SHAMPOO_TWO) * jnp.einsum(
        "tij,tkj->tik", grad, grad, precision=HIGH
    )
    new_right = SHAMPOO_TWO * right + (1.0 - SHAMPOO_TWO) * jnp.einsum(
        "tji,tjk->tik", grad, grad, precision=HIGH
    )
    new_moment = SHAMPOO_ONE * moment + (1.0 - SHAMPOO_ONE) * grad
    halfway = jnp.einsum("tij,tjk->tik", left_inv, new_moment, precision=HIGH)
    direction = jnp.einsum("tij,tjk->tik", halfway, right_inv, precision=HIGH)
    new_master = master - SHAMPOO_RATE * (direction + SHAMPOO_DECAY * master)
    return (new_moment, new_left, new_right, new_master)


def local(
    latents,
    noise,
    timesteps,
    labels,
    grid,
    flat_master,
    flat_moment,
    flat_second,
    tile_master,
    tile_moment,
    tile_left,
    tile_right,
    left_root,
    right_root,
):
    x, y, z, c = [lax.axis_index(name) for name in ("x", "y", "z", "c")]
    groups = lax.axis_size("z") * lax.axis_size("y")
    ranks = lax.axis_size("x") * lax.axis_size("c")
    count_tiles = tile_master.shape[1]
    simple = lax.axis_size("y") == 2 and lax.axis_size("z") == 4 and count_tiles == 12
    ranks_here = [2 * x + c, 2 * (1 - x) + c]
    number = (z * lax.axis_size("y") + y) * 2 + x

    owner = z * lax.axis_size("y") + y
    if simple:
        is_mixer = owner % 4 == 0
        strip = strips_of(tile_master[0].astype(BF16), is_mixer)[0]
        planes = gather_strips(strip)
    else:
        planes = gather_any(tile_master[0].astype(BF16))
    mats = []
    for layer in range(LAYERS):
        per_rank = []
        for i in range(2):
            (mixer, mid), (low, last) = planes[2 * layer][i], planes[2 * layer + 1][i]
            per_rank.append(
                (
                    mixer,
                    mid[:BLK],
                    jnp.concatenate([mid[BLK:], low[: 2 * BLK]]),
                    jnp.concatenate([low[2 * BLK :], last]),
                )
            )
        mats.append(per_rank)

    info = jnp.concatenate(
        [timesteps[:, 0], labels[:, 0], grid[:, 0, 0], grid[:, 1, 0]]
    ).reshape(1, 4, MB)
    info = gather_rows(info, ("y", "z"))
    info = info.transpose(1, 0, 2).reshape(4, groups * MB)
    count = jnp.sum((info[2] * info[3]).astype(F32))
    height = lax.dynamic_index_in_dim(info[2], number, 0, keepdims=False)
    width = lax.dynamic_index_in_dim(info[3], number, 0, keepdims=False)
    patches = own_sequence(latents)
    target = own_sequence(noise)
    rows = patches.shape[1]
    slots = jnp.arange(rows)
    valid = slots < height * width

    flat = Flat(flat_master.shape[0])
    held = flat.align(flat_master.astype(BF16))
    held_f32 = held.astype(F32)
    small = jnp.concatenate(
        [flat.take(held_f32, 0, ROW_STEM)]
        + [flat.take(held_f32, BASE_B1, ROW_D), flat.take(held_f32, BASE_B2, ROW_D)]
        + [
            flat.take(held_f32, BASE_LAYER + l * LAYER_ROWS + D * ROW_ADA, ROW_BIAS)
            for l in range(LAYERS)
        ]
        + [flat.take(held_f32, BASE_TAIL, ROW_TAIL)]
    )
    small = all_sum(small.astype(BF16)).astype(F32)
    pieces = []
    at = 0
    for amount in [ROW_STEM, ROW_D, ROW_D] + [ROW_BIAS] * LAYERS + [ROW_TAIL]:
        pieces.append(small[at : at + amount].reshape(-1))
        at = at + amount
    stem, time_b1, time_b2 = pieces[:3]
    tail = pieces[-1]
    patch_w, patch_b = stem[: PATCH * D].reshape(PATCH, D), stem[PATCH * D :]
    final_b, head_w = tail[: 2 * D], tail[2 * D :].reshape(D, PATCH).astype(BF16)
    biases, ada_bs = ([], [])
    for layer in range(LAYERS):
        vector = pieces[3 + layer]
        ada_bs.append(vector[: 6 * D])
        biases.append(jnp.split(vector[6 * D :], [3 * D, 4 * D, 8 * D]))

    freq = jax.vmap(time_freq)(info[0])
    onehot = (jnp.arange(CLASSES)[None, :] == info[1][:, None]).astype(F32)
    hidden_pre = (
        all_sum(flat.product(held_f32, freq, BASE_W1, ROW_D, HIGH)) + time_b1
    )
    hidden = jax.nn.silu(hidden_pre)
    cond = flat.product(held_f32, hidden, BASE_W2, ROW_D, HIGH)
    cond = cond + flat.product(held_f32, onehot, BASE_TABLE, ROW_D)
    cond = all_sum(cond) + time_b2
    cond_s = jax.nn.silu(cond).astype(BF16)
    mods = jnp.concatenate(
        [
            flat.product(held, cond_s, BASE_LAYER + l * LAYER_ROWS, ROW_ADA)
            for l in range(LAYERS)
        ]
        + [flat.product(held, cond_s, BASE_FINAL, ROW_FINAL)],
        axis=1,
    )
    mods = all_sum(scatter_rows(mods, ("z", "y", "x")), ("c",))[0]
    modulations = [mods[l * 6 * D : (l + 1) * 6 * D] + ada_bs[l] for l in range(LAYERS)]
    final_mod = mods[LAYERS * 6 * D :] + final_b

    state = contract_rows(patches, patch_w.astype(BF16)) + patch_b + place_embed(slots, width)
    kept = [None] * LAYERS
    for layer in range(LAYERS):
        state, kept[layer] = layer_forward(
            state, modulations[layer], biases[layer], mats[layer], valid, ranks_here, ranks
        )
    shift_f, scale_f = jnp.split(final_mod, 2)
    normed_f = modulate(state, shift_f, scale_f).astype(BF16)
    predicted = jnp.dot(normed_f, head_w, preferred_element_type=F32)
    error = predicted - target.T
    loss_part = jnp.sum(jnp.where(valid[:, None], error * error, 0.0))
    grad_pred = jnp.where(valid[:, None], 2.0 * error / (PATCH * count), 0.0).astype(BF16)

    grad_head = contract_rows(normed_f, grad_pred)
    grad_normed_f = contract_cols(grad_pred, head_w)
    unused, pull_f = jax.vjp(modulate, state, shift_f, scale_f)
    grad_state, grad_shift_f, grad_scale_f = pull_f(grad_normed_f)
    grad_final = jnp.concatenate([grad_shift_f, grad_scale_f])
    grad_mods, grad_biases = ([None] * LAYERS, [None] * LAYERS)
    grad_planes = [None] * 4
    for layer in reversed(range(LAYERS)):
        grad_state, grad_mods[layer], grad_biases[layer], both = layer_backward(
            grad_state, modulations[layer], mats[layer], kept[layer], valid, ranks_here, ranks
        )
        grad_planes[2 * layer], grad_planes[2 * layer + 1] = both
    if simple:
        mine = None
        for plane in reversed(range(4)):
            halves = [reduce_line(part, plane) for part in reduce_plane(grad_planes[plane])]
            whole = jnp.concatenate(halves)
            mine = whole if mine is None else jnp.where(z == plane, whole, mine)
        grad_tiles = tiles_of(mine[None], is_mixer).astype(F32)
    else:
        grad_tiles = reduce_any(grad_planes, count_tiles).astype(F32)
    grad_patch_b = jnp.sum(grad_state, axis=0)
    grad_patch_w = jnp.dot(patches.astype(F32), grad_state, precision=HIGH)
    once = jnp.where(c == 0, 1.0, 0.0)
    summed = jnp.concatenate(
        [grad_patch_w.reshape(-1) * once, grad_patch_b * once]
        + grad_biases
        + [grad_head.reshape(-1) * once, jnp.pad(loss_part[None] * once, (0, LANE - 1))]
    )
    summed = all_sum(summed.reshape(-1, LANE))
    stem_rows = summed[:ROW_STEM]
    extra = ROW_BIAS - ROW_ADA
    bias_rows = [summed[ROW_STEM + l * extra : ROW_STEM + (l + 1) * extra] for l in range(LAYERS)]
    head_rows = summed[ROW_STEM + LAYERS * extra : -1]
    summed_loss = summed[-1, 0]

    all_mods = gather_rows(
        jnp.concatenate(grad_mods + [grad_final])[None], ("x", "y", "z")
    )
    mods_of = [all_mods[:, l * 6 * D : (l + 1) * 6 * D] for l in range(LAYERS)]
    final_of = all_mods[:, LAYERS * 6 * D :]
    grad_cond = flat.back_product(held, final_of, BASE_FINAL, ROW_FINAL, D)
    for layer in range(LAYERS):
        grad_cond = grad_cond + flat.back_product(
            held, mods_of[layer], BASE_LAYER + layer * LAYER_ROWS, ROW_ADA, D
        )
    grad_cond = all_sum(grad_cond)
    grad_cond = jax.vjp(jax.nn.silu, cond)[1](grad_cond)[0]
    grad_hidden = all_sum(flat.back_product(held, grad_cond, BASE_W2, ROW_D, D))
    grad_hidden = jax.vjp(jax.nn.silu, hidden_pre)[1](grad_hidden)[0]

    def total_rows(values):
        return jnp.sum(values, axis=0).reshape(-1, LANE)

    cond_f = cond_s.astype(F32)
    out = jnp.zeros((flat.total, LANE), F32)
    out = flat.put_rows(out, stem_rows, 0)
    out = flat.put_outer(out, freq, grad_hidden, BASE_W1, ROW_D)
    out = flat.put_rows(out, total_rows(grad_hidden), BASE_B1)
    out = flat.put_outer(out, hidden, grad_cond, BASE_W2, ROW_D)
    out = flat.put_rows(out, total_rows(grad_cond), BASE_B2)
    out = flat.put_outer(out, onehot, grad_cond, BASE_TABLE, ROW_D)
    for layer in range(LAYERS):
        base = BASE_LAYER + layer * LAYER_ROWS
        out = flat.put_outer(out, cond_f, mods_of[layer], base, ROW_ADA)
        vector = jnp.concatenate([total_rows(mods_of[layer]), bias_rows[layer]])
        out = flat.put_rows(out, vector, base + D * ROW_ADA)
    out = flat.put_outer(out, cond_f, final_of, BASE_FINAL, ROW_FINAL)
    out = flat.put_rows(out, jnp.concatenate([total_rows(final_of), head_rows]), BASE_TAIL)
    grad_flat = flat.unalign(out)

    square = jnp.sum(grad_flat * grad_flat) + jnp.sum(grad_tiles * grad_tiles)
    norm = jnp.sqrt(all_sum(square.reshape(1, 1))[0, 0])
    factor = jnp.minimum(1.0, CLIP_AT / (norm + 1e-06))
    new_moment, new_second, new_flat = adamw(
        grad_flat * factor, flat_moment, flat_second, flat_master
    )
    tile_mom, new_left, new_right, new_tiles = shampoo(
        grad_tiles * factor,
        tile_moment[0],
        tile_left[0],
        tile_right[0],
        left_root[0],
        right_root[0],
        tile_master[0],
    )
    return (
        summed_loss,
        count,
        norm,
        new_moment,
        new_second,
        new_flat,
        tile_mom[None],
        new_left[None],
        new_right[None],
        new_tiles[None],
    )


def solution(mesh):
    deep = 4
    axes = Mesh(
        mesh.devices.reshape(deep, mesh.shape["dp"] // deep, MB, mesh.shape["mp"] // MB),
        ("z", "y", "x", "c"),
    )
    dp, mp, whole = ("z", "y"), ("x", "c"), ("z", "y", "x", "c")
    tile = P(mp, dp, None, None)
    in_specs = (
        P(None, None, whole),
        P(None, None, whole),
        P(None, dp),
        P(None, dp),
        P(None, None, dp),
        P(whole),
        P(whole),
        P(whole),
    ) + (tile,) * 6
    out_specs = (P(), P(), P(), P(whole), P(whole), P(whole)) + (tile,) * 4
    return jax.shard_map(local, mesh=axes, in_specs=in_specs, out_specs=out_specs, check_vma=False)
```

```python
import functools
import math

import jax
import jax.numpy as jnp
from jax import lax
from jax.experimental import pallas as pl
from jax.experimental.pallas import tpu as pltpu
from jax.sharding import Mesh
from jax.sharding import PartitionSpec as P

D = 1152
HD = 72
FF = 4608
PATCH = 16
FREQ = 256
CLASSES = 1000
BLK = 288
LAYERS = 2
STEP_COUNT = 10
MB = 2
SIDE = 32
LANE = 128
STRIP = 3 * BLK


HIGH = lax.Precision.HIGHEST
NORM_EPS = 1e-06
CLIP_AT = 0.005
ADAM_ONE = 0.9
ADAM_TWO = 0.999
ADAM_EPS = 1e-08
ADAM_RATE = 0.02
ADAM_DECAY = 0.01
SHAMPOO_ONE = 0.9
SHAMPOO_TWO = 0.99
SHAMPOO_RATE = 0.01
SHAMPOO_DECAY = 0.01

F32 = jnp.float32
BF16 = jnp.bfloat16
SWAP = [(0, 1), (1, 0)]
LOG2E = 1.4426950408889634
SCALE = HD ** (-0.5)
SC2 = SCALE * LOG2E
HEADS_HERE = 4
WIDE = HD * HEADS_HERE

ROW_D = D // LANE
ROW_STEM = (PATCH + 1) * ROW_D
BASE_W1 = ROW_STEM
BASE_B1 = BASE_W1 + FREQ * ROW_D
BASE_W2 = BASE_B1 + ROW_D
BASE_B2 = BASE_W2 + D * ROW_D
BASE_TABLE = BASE_B2 + ROW_D
BASE_LAYER = BASE_TABLE + CLASSES * ROW_D
ROW_ADA = 6 * ROW_D
ROW_BIAS = (6 + 3 + 1 + 4 + 1) * ROW_D
LAYER_ROWS = D * ROW_ADA + ROW_BIAS
BASE_FINAL = BASE_LAYER + LAYERS * LAYER_ROWS
ROW_FINAL = 2 * ROW_D
BASE_TAIL = BASE_FINAL + D * ROW_FINAL
ROW_TAIL = ROW_FINAL + PATCH * ROW_D
FRONT = 56


def time_freq(step):
    half = FREQ // 2
    freqs = jnp.exp(-math.log(10000.0) * jnp.arange(half).astype(F32) / half)
    angles = step.astype(F32) * freqs
    return jnp.concatenate([jnp.cos(angles), jnp.sin(angles)])


def place_embed(slots, width):
    quarter = D // 4
    omega = jnp.power(10000.0, -jnp.arange(quarter).astype(F32) / quarter)
    angle = jnp.arange(SIDE).astype(F32)[:, None] * omega
    table = jnp.concatenate([jnp.sin(angle), jnp.cos(angle)], axis=1)
    places = jnp.arange(SIDE)[None]
    row = ((slots // width)[:, None] == places).astype(F32)
    col = ((slots % width)[:, None] == places).astype(F32)
    return jnp.concatenate(
        [jnp.dot(row, table, precision=HIGH), jnp.dot(col, table, precision=HIGH)], axis=1
    )


def normalize(state):
    centered = state - jnp.mean(state, axis=-1, keepdims=True)
    spread = jnp.mean(centered * centered, axis=-1, keepdims=True)
    return centered * lax.rsqrt(spread + NORM_EPS)


def modulate(state, shift, scale):
    return normalize(state) * (1.0 + scale) + shift


def gelu_tanh(value):
    return jax.nn.gelu(value, approximate=True)


def contract_rows(left, right):
    return lax.dot_general(left, right, (((0,), (0,)), ((), ())), preferred_element_type=F32)


def contract_cols(left, right):
    return lax.dot_general(left, right, (((1,), (1,)), ((), ())), preferred_element_type=F32)


def size_of(axes):
    size = 1
    for axis in axes:
        size = size * lax.axis_size(axis)
    return size


def index_of(axes):
    index = 0
    for axis in axes:
        index = index * lax.axis_size(axis) + lax.axis_index(axis)
    return index


def from_others(pick, axes):
    size = size_of(axes)
    return [pick(0)] + [
        lax.ppermute(pick(k), axes, [(i, i ^ k) for i in range(size)]) for k in range(1, size)
    ]


def tree_sum(values):
    while len(values) > 1:
        values = [values[i] + values[i + 1] for i in range(0, len(values), 2)]
    return values[0]


def all_sum(value, groups=(("c",), ("y", "x"), ("z",))):
    for axes in groups:
        value = tree_sum(from_others(lambda k: value, axes))
    return value


def gather_rows(value, groups):
    for axes in groups:
        found = jnp.stack(from_others(lambda k: value, axes))
        size, me = size_of(axes), index_of(axes)
        bit = 1
        while bit < size:
            pairs = found.reshape((size // (2 * bit), 2, bit) + value.shape)
            found = jnp.where((me & bit) == 0, pairs, pairs[:, ::-1]).reshape(found.shape)
            bit *= 2
        value = found.reshape((-1,) + value.shape[1:])
    return value


def scatter_rows(value, axes):
    size, me = size_of(axes), index_of(axes)
    parts = value.reshape((size, -1) + value.shape[1:])
    return tree_sum(
        from_others(lambda k: lax.dynamic_index_in_dim(parts, me ^ k, 0, keepdims=False), axes)
    )


def columns_by_core(value):
    parts = value.reshape(value.shape[:-1] + (2, -1))
    c = lax.axis_index("c")
    keep = lax.dynamic_index_in_dim(parts, c, -2, keepdims=False)
    send = lax.dynamic_index_in_dim(parts, 1 - c, -2, keepdims=False)
    return keep + lax.ppermute(send, "c", SWAP)


def columns_of_cores(value):
    other = lax.ppermute(value, "c", SWAP)
    c = lax.axis_index("c")
    return jnp.where(
        c == 0, jnp.concatenate([value, other], -1), jnp.concatenate([other, value], -1)
    )


def own_sequence(values):
    x = lax.axis_index("x")
    send = lax.dynamic_index_in_dim(values, 1 - x, 0, keepdims=False)
    keep = lax.dynamic_index_in_dim(values, x, 0, keepdims=False)
    other = lax.ppermute(send, "x", SWAP)
    pair = jnp.where(x == 0, jnp.stack([keep, other]), jnp.stack([other, keep]))
    more = lax.ppermute(pair, "c", SWAP)
    both = jnp.where(
        lax.axis_index("c") == 0, jnp.stack([pair, more], 1), jnp.stack([more, pair], 1)
    )
    return both.transpose(2, 0, 1, 3).reshape(values.shape[1], -1)


def strips_of(tiles, is_mixer):
    count = tiles.shape[0] // 12
    plain = (
        tiles.reshape(count, 3, 4, BLK, BLK).transpose(0, 1, 3, 2, 4).reshape(count, STRIP, D)
    )
    turned = (
        tiles.reshape(count, 4, 3, BLK, BLK).transpose(0, 2, 4, 1, 3).reshape(count, STRIP, D)
    )
    return jnp.where(is_mixer, turned, plain)


def tiles_of(strips, is_mixer):
    count = strips.shape[0]
    plain = (
        strips.reshape(count, 3, BLK, 4, BLK).transpose(0, 1, 3, 2, 4).reshape(-1, BLK, BLK)
    )
    turned = (
        strips.reshape(count, 3, BLK, 4, BLK).transpose(0, 3, 1, 4, 2).reshape(-1, BLK, BLK)
    )
    return jnp.where(is_mixer, turned, plain)


def select_y(own, other):
    first = lax.axis_index("y") == 0
    return jnp.where(first, own, other), jnp.where(first, other, own)


HALF = STRIP // 2


class Overlap:
    def __init__(self):
        self.before = []
        self.source = None
        self.moves = []

    def feed(self, source):
        self.source = source
        self.advance(None)

    def advance(self, got):
        try:
            self.moves = self.source.send(got)
        except StopIteration:
            self.source = None
            self.moves = []

    def beside(self, work, *carry):
        values = [move[0] for move in self.moves]
        unused, values, carry = lax.optimization_barrier((self.before, values, carry))
        got = [lax.ppermute(value, move[1], move[2]) for value, move in zip(values, self.moves)]
        result = work(*carry)
        self.before = got
        if self.source is not None:
            self.advance(got)
        return result

    def alone(self, work, *carry):
        self.before, carry = lax.optimization_barrier((self.before, carry))
        result = work(*carry)
        self.before = [jax.tree.leaves(result), self.before]
        return result


def by_plane(options):
    z = lax.axis_index("z")
    chosen = None
    for place, value in options.items():
        chosen = value if chosen is None else jnp.where(z == place, value, chosen)
    return chosen


PARTS = [(0, 176), (176, 160), (336, 176), (512, 160)]
LATE = (672, 192)
HALVES = [(672, 96), (768, 96)]


def place():
    return [lax.axis_index(name) for name in ("z", "y", "x", "c")]


def meet(devices):
    barrier = pltpu.get_barrier_semaphore()
    z = lax.axis_index("z")
    amount = 2
    for key, device in devices.items():
        if key in ("up", "down"):
            there = (z < 3) if key == "up" else (z > 0)

            @pl.when(there)
            def signal(device=device):
                pl.semaphore_signal(barrier, 1, device_id=device, device_id_type=pl.DeviceIdType.MESH)

            amount = amount + there.astype(jnp.int32)
        else:
            pl.semaphore_signal(barrier, 1, device_id=device, device_id_type=pl.DeviceIdType.MESH)
    pl.semaphore_wait(barrier, amount)


def neighbours():
    z, y, x, c = place()
    return {
        "x": (z, y, 1 - x, c),
        "y": (z, 1 - y, x, c),
        "up": (jnp.minimum(z + 1, 3), y, x, c),
        "down": (jnp.maximum(z - 1, 0), y, x, c),
    }


def gather_kernel(strip_ref, out_ref, own_sem, send_z, recv_z, send_p, recv_p, send_c, recv_c):
    z, y, x, c = place()
    device = neighbours()
    meet(device)

    def region(far, plane, yi, rows):
        at = pl.multiple_of((2 * plane + yi) * STRIP + rows[0], 16)
        return out_ref.at[far, pl.ds(at, rows[1]), :]

    def copy(far, plane, yi, rows, key, send, recv):
        return pltpu.make_async_remote_copy(
            src_ref=region(far, plane, yi, rows),
            dst_ref=region(1 - far if key == "x" else far, plane, yi, rows),
            send_sem=send,
            recv_sem=recv,
            device_id=device[key],
            device_id_type=pl.DeviceIdType.MESH,
        )

    own = pltpu.make_async_copy(strip_ref, region(0, z, y, (0, STRIP)), own_sem)
    own.start()

    def valid(d):
        if d == 0:
            return None
        return (z >= d) if d > 0 else (z <= 3 + d)

    def run(condition, action):
        if condition is None:
            action()
        else:
            pl.when(condition)(action)

    def plane_copies(d, p, rows, first):
        second = "y" if first == "x" else "x"
        plane = z - d
        sems = [(send_p.at[d + 3, p, hop], recv_p.at[d + 3, p, hop]) for hop in range(3)]
        hop1 = copy(0, plane, y, rows, first, *sems[0])
        hop2 = copy(0, plane, y, rows, second, *sems[1])
        got = (1, y) if first == "x" else (0, 1 - y)
        hop3 = copy(got[0], plane, got[1], rows, second, *sems[2])
        return hop1, hop2, hop3

    def z_copy(d, p, key):
        index = d + 3
        nxt = index + 1 if key == "up" else index - 1
        slot = 0 if key == "up" else 1
        return copy(0, z - d, y, PARTS[p], key, send_z.at[index, p, slot], recv_z.at[nxt, p])

    def z_wait(d, p):
        key = "down" if d > 0 else "up"
        copy(0, z - d, y, PARTS[p], key, send_z.at[3, p, 0], recv_z.at[d + 3, p]).wait_recv()

    firsts = ["x", "y", "x", "y"]
    events = sorted(
        [(d, p) for d in range(-3, 4) for p in range(4)], key=lambda e: (abs(e[0]) + e[1], abs(e[0]))
    )
    lag = 16
    todo = []

    def forward(d, p):
        hop1, hop2, hop3 = plane_copies(d, p, PARTS[p], firsts[p])

        def action():
            hop1.wait_recv()
            hop3.start()

        run(valid(d), action)

    own.wait()
    for h in range(2):
        hop1, hop2, hop3 = plane_copies(0, 4 + h, HALVES[h], firsts[h])
        hop1.start()
        hop2.start()
    for number, (d, p) in enumerate(events):

        def action(d=d, p=p):
            if d != 0:
                z_wait(d, p)
            if d >= 0:
                run(z < 3, lambda: z_copy(d, p, "up").start())
            if d <= 0:
                run(z > 0, lambda: z_copy(d, p, "down").start())
            hop1, hop2, hop3 = plane_copies(d, p, PARTS[p], firsts[p])
            hop1.start()
            hop2.start()

        run(valid(d), action)
        if number == 3:
            for h in range(2):
                hop1, hop2, hop3 = plane_copies(0, 4 + h, HALVES[h], firsts[h])
                hop1.wait_recv()
                hop3.start()
        todo.append((d, p))
        if len(todo) > lag:
            forward(*todo.pop(0))

    def late(d, xi, yi, key):
        index = d + 3
        nxt = index + 1 if key == "up" else index - 1
        slot = 0 if key == "up" else 1
        k = 2 * xi + yi
        return copy(xi, z - d, yi, LATE, key, send_c.at[index, k, slot], recv_c.at[nxt, k])

    def late_wait(d, xi, yi):
        key = "down" if d > 0 else "up"
        k = 2 * xi + yi
        copy(xi, z - d, yi, LATE, key, send_c.at[3, 0, 0], recv_c.at[d + 3, k]).wait_recv()

    for h in range(2):
        unused, hop2, hop3 = plane_copies(0, 4 + h, HALVES[h], firsts[h])
        hop2.wait_recv()
        hop3.wait_recv()
    for distance in range(4):
        for xi in range(2):
            for yi in range(2):
                for d in ([0] if distance == 0 else [distance, -distance]):

                    def action(d=d, xi=xi, yi=yi):
                        if d != 0:
                            late_wait(d, xi, yi)
                        if d >= 0 and d < 3:
                            run(z < 3, lambda: late(d, xi, yi, "up").start())
                        if d <= 0 and d > -3:
                            run(z > 0, lambda: late(d, xi, yi, "down").start())

                    run(valid(d), action)
                if todo:
                    forward(*todo.pop(0))
    while todo:
        forward(*todo.pop(0))

    for d, p in events:

        def action(d=d, p=p):
            hop1, hop2, hop3 = plane_copies(d, p, PARTS[p], firsts[p])
            hop2.wait_recv()
            hop3.wait_recv()
            hop1.wait_send()
            hop2.wait_send()
            hop3.wait_send()
            if d >= 0:
                run(z < 3, lambda: z_copy(d, p, "up").wait_send())
            if d <= 0:
                run(z > 0, lambda: z_copy(d, p, "down").wait_send())

        run(valid(d), action)
    for h in range(2):
        hop1, hop2, hop3 = plane_copies(0, 4 + h, HALVES[h], firsts[h])
        hop1.wait_send()
        hop2.wait_send()
        hop3.wait_send()
    for d in range(-3, 4):
        for xi in range(2):
            for yi in range(2):

                def action(d=d, xi=xi, yi=yi):
                    if d >= 0 and d < 3:
                        run(z < 3, lambda: late(d, xi, yi, "up").wait_send())
                    if d <= 0 and d > -3:
                        run(z > 0, lambda: late(d, xi, yi, "down").wait_send())

                run(valid(d), action)


def gather_strips(strip):
    return pl.pallas_call(
        gather_kernel,
        out_shape=jax.ShapeDtypeStruct((2, 8 * STRIP, D), BF16),
        in_specs=[pl.BlockSpec(memory_space=pl.ANY)],
        out_specs=pl.BlockSpec(memory_space=pl.ANY),
        scratch_shapes=[
            pltpu.SemaphoreType.DMA,
            pltpu.SemaphoreType.DMA((7, 4, 2)),
            pltpu.SemaphoreType.DMA((7, 4)),
            pltpu.SemaphoreType.DMA((7, 6, 3)),
            pltpu.SemaphoreType.DMA((7, 6, 3)),
            pltpu.SemaphoreType.DMA((7, 4, 2)),
            pltpu.SemaphoreType.DMA((7, 4)),
        ],
        compiler_params=pltpu.CompilerParams(collective_id=1, has_side_effects=True),
        name="gather_strips",
    )(strip)


def gather_any(tiles, planes):
    whole = lax.all_gather(tiles, ("z", "y", "x"), axis=0, tiled=False)
    x = lax.axis_index("x")
    whole = whole.reshape((-1, 2) + tiles.shape)
    groups = []
    for place in (x, 1 - x):
        blocks = lax.dynamic_index_in_dim(whole, place, 1, keepdims=False)
        blocks = blocks.reshape(-1, BLK, BLK)
        groups.append(strips_of(blocks, (jnp.arange(8) % 4 == 0)[:, None, None]))
    for plane in range(4):
        planes[plane] = [(groups[i][2 * plane], groups[i][2 * plane + 1]) for i in range(2)]


def add_low(left, right):
    return (left.astype(F32) + right.astype(F32)).astype(BF16)


def line_moves(parts, plane, done):
    parts = list(parts)
    rights, lefts = plane, 3 - plane
    hops = max(rights, lefts)
    for step in range(hops + 1):
        moves, which = [], []
        for i in range(2):
            hop = step - i
            if 0 <= hop < hops:
                if hop < rights:
                    moves.append((parts[i], "z", [(hop, hop + 1)]))
                    which.append(i)
                if hop < lefts:
                    moves.append((parts[i], "z", [(3 - hop, 2 - hop)]))
                    which.append(i)
        got = yield moves
        for i, value in zip(which, got):
            parts[i] = add_low(parts[i], value)
    done[plane] = jnp.concatenate(parts)
    yield None


def reduce_strips(planes, done):
    y = lax.axis_index("y")
    lines = []

    def pick(pair, own):
        first = (y == 0) if own else (y == 1)
        return jnp.where(first, pair[0], pair[1])

    def everything(moves):
        whole = list(moves)
        spans = []
        for line in lines:
            spans.append((line, len(whole), len(whole) + len(line[1])))
            whole += line[1]
        return whole, spans

    def settle(got, spans):
        for line, begin, end in spans:
            line[1] = line[0].send(got[begin:end])
            if line[1] is None:
                lines.remove(line)

    for plane in (3, 2, 1, 0):
        grads = planes[plane]
        send_x = jnp.stack([part[:HALF] for part in grads[1]])
        lows = [[part[HALF:] for part in group] for group in grads]
        send_y = jnp.stack([pick(group, False) for group in lows])
        moves, spans = everything([(send_x, "x", SWAP), (send_y, "y", SWAP)])
        got = yield moves
        settle(got, spans)
        upper = [add_low(grads[0][i][:HALF], got[0][i]) for i in range(2)]
        lower = [add_low(pick(lows[i], True), got[1][i]) for i in range(2)]
        moves, spans = everything([(pick(upper, False), "y", SWAP), (lower[1], "x", SWAP)])
        got = yield moves
        settle(got, spans)
        parts = [add_low(pick(upper, True), got[0]), add_low(lower[0], got[1])]
        line = line_moves(parts, plane, done)
        lines.append([line, next(line)])
        if plane % 2 == 1:
            moves, spans = everything([])
            got = yield moves
            settle(got, spans)
    while lines:
        moves, spans = everything([])
        got = yield moves
        settle(got, spans)


def reduce_any(planes, count):
    x = lax.axis_index("x")
    groups = []
    for place in range(2):
        chosen = [
            jnp.where(x == place, planes[plane][0][y], planes[plane][1][y])
            for plane in range(4)
            for y in range(2)
        ]
        blocks = tiles_of(jnp.stack(chosen), jnp.zeros((), bool)).reshape(8, 12, BLK, BLK)
        turned = tiles_of(jnp.stack(chosen), jnp.ones((), bool)).reshape(8, 12, BLK, BLK)
        mixer = (jnp.arange(8) % 4 == 0)[:, None, None, None]
        groups.append(jnp.where(mixer, turned, blocks).reshape(-1, count, BLK, BLK))
    whole = jnp.stack(groups, axis=1).reshape(-1, BLK, BLK)
    return lax.psum_scatter(whole, ("z", "y", "x"), scatter_dimension=0, tiled=True)


def pad_to(value, step):
    return -(-value // step) * step


def piece_at(first, base, width, height):
    skip = jnp.minimum(jnp.maximum(first - base, 0) // width, height)
    return skip, base + skip * width - first + FRONT


def split_dot(left, right, dims):
    return lax.dot_general(
        left, right, (dims, ((), ())), precision=HIGH, preferred_element_type=F32
    )


class Flat:
    def __init__(self, length):
        start = index_of(("z", "y", "x", "c")) * length
        self.length = length
        self.where = jnp.stack([start // LANE, start % LANE]).astype(jnp.int32)
        self.packed = pad_to(-(-length // LANE), 8)
        self.rows = self.packed + 8
        self.total = FRONT + self.rows + pad_to(self.rows + 3 * ROW_ADA * 8, 8)

    def count(self, width, height):
        return pad_to(min(height, self.rows // width + 2), 8)

    def call(self, body, outs, operands, scratch=(), name="flat"):
        def kernel(where, *refs):
            body(where[0], where[1], *refs)

        amount = len(operands)
        return pl.pallas_call(
            kernel,
            out_shape=outs,
            in_specs=[pl.BlockSpec(memory_space=pltpu.SMEM)]
            + [pl.BlockSpec(memory_space=pltpu.VMEM)] * amount,
            out_specs=jax.tree.map(lambda v: pl.BlockSpec(memory_space=pltpu.VMEM), outs),
            scratch_shapes=list(scratch),
            compiler_params=pltpu.CompilerParams(vmem_limit_bytes=52 * 1024 * 1024),
            name=name,
        )(self.where, *operands)

    def when_here(self, first, piece, action):
        base, width, height = piece
        skip, at = piece_at(first, base, width, height)

        @pl.when((skip < height) & (at < FRONT + self.rows))
        def run():
            action(skip, at)

    def padded(self, factor, width):
        count = self.count(width, factor.shape[1])
        return jnp.pad(factor.astype(F32).T, ((0, count), (0, 0)))

    def align(self, shard):
        flat = jnp.pad(shard, (0, self.packed * LANE - self.length)).reshape(self.packed, LANE)

        def body(first, skew, flat_ref, held_ref):
            held_ref[:FRONT] = jnp.zeros((FRONT, LANE), F32)
            values = flat_ref[...].astype(BF16).astype(F32)
            turned = pltpu.roll(values, skew, 1)
            lanes = lax.broadcasted_iota(jnp.int32, (self.packed, LANE), 1)
            empty = jnp.zeros((8, LANE), F32)
            here = jnp.where(lanes >= skew, turned, 0.0)
            carry = jnp.where(lanes >= skew, 0.0, turned)
            held_ref[FRONT : FRONT + self.packed] = here
            held_ref[FRONT + self.packed :] = jnp.zeros(
                (self.total - FRONT - self.packed, LANE), F32
            )
            held_ref[FRONT + 1 : FRONT + 1 + self.packed] += carry

        return self.call(
            body, jax.ShapeDtypeStruct((self.total, LANE), F32), [flat], name="align"
        )

    def take(self, held, pieces):
        amount = sum(height for base, height in pieces)
        size = pad_to(2 * amount, 8)

        def body(first, skew, held_ref, out_ref):
            out_ref[...] = jnp.zeros_like(out_ref)
            put = 0
            for base, height in pieces:

                def action(skip, at, put=put, height=height):
                    block = held_ref[pl.ds(at, height), :]
                    index = lax.broadcasted_iota(jnp.int32, (height, LANE), 0)
                    out_ref[pl.ds(put + skip, height), :] = jnp.where(
                        index < height - skip, block, 0.0
                    )

                self.when_here(first, (base, 1, height), action)
                put += height

        out = self.call(body, jax.ShapeDtypeStruct((size, LANE), F32), [held], name="take")
        return out[:amount]

    def product(self, held, factors, pieces, exact, join):
        operands = [self.padded(f, piece[1]) for f, piece in zip(factors, pieces)]
        number = factors[0].shape[0]
        wide = [piece[1] * LANE for piece in pieces]
        out = jax.ShapeDtypeStruct((number, wide[0] if join else sum(wide)), F32)

        def body(first, skew, held_ref, *refs):
            out_ref = refs[-1]
            out_ref[...] = jnp.zeros_like(out_ref)
            put = 0
            for piece, factor_ref in zip(pieces, refs[:-1]):
                base, width, height = piece
                count = self.count(width, height)

                def action(skip, at, width=width, count=count, factor_ref=factor_ref, put=put):
                    near = factor_ref[pl.ds(skip, count), :]
                    near = near if exact else near.astype(BF16)
                    for u in range(width):
                        block = held_ref[pl.ds(at + u, count, stride=width), :]
                        if exact:
                            value = split_dot(near, block, ((0,), (0,)))
                        else:
                            value = contract_rows(near, block.astype(BF16))
                        out_ref[:, put + u * LANE : put + (u + 1) * LANE] += value

                self.when_here(first, piece, action)
                put = put if join else put + width * LANE

        return self.call(body, out, [held] + operands, name="product")

    def back_product(self, held, grads, pieces):
        number, height = grads[0].shape[0], pieces[0][2]
        most = max(self.count(piece[1], height) for piece in pieces)

        def body(first, skew, held_ref, *refs):
            out_ref = refs[-1]
            out_ref[...] = jnp.zeros_like(out_ref)
            for piece, grad_ref in zip(pieces, refs[:-1]):
                width = piece[1]
                count = self.count(width, height)

                def action(skip, at, width=width, count=count, grad_ref=grad_ref):
                    value = jnp.zeros((count, number), F32)
                    for u in range(width):
                        block = held_ref[pl.ds(at + u, count, stride=width), :]
                        grad = grad_ref[:, u * LANE : (u + 1) * LANE]
                        value = value + split_dot(block, grad, ((1,), (1,)))
                    out_ref[pl.ds(skip, count), :] += value

                self.when_here(first, piece, action)

        out = self.call(
            body,
            jax.ShapeDtypeStruct((height + most, number), F32),
            [held] + list(grads),
            name="back_product",
        )
        return out[:height].T

    def gradient(self, parts):
        operands, plan = ([], [])
        for part in parts:
            if len(part) == 2:
                base, values = part
                height = values.shape[0]
                operands.append(jnp.pad(values, ((0, height), (0, 0))))
                plan.append((base, 1, height, len(operands) - 1, None))
            else:
                base, width, left, right = part
                operands += [self.padded(left, width), right]
                plan.append((base, width, left.shape[1], len(operands) - 2, len(operands) - 1))

        def body(first, skew, *refs):
            grad_ref, square_ref, rows_ref = refs[-3:]
            for base, width, height, one, two in plan:

                def vector(skip, at, height=height, one=one):
                    rows_ref[pl.ds(at, height), :] = refs[one][pl.ds(skip, height), :]

                def outer(skip, at, width=width, height=height, one=one, two=two):
                    count = self.count(width, height)
                    near = refs[one][pl.ds(skip, count), :]
                    for u in range(width):
                        grad = refs[two][:, u * LANE : (u + 1) * LANE]
                        rows_ref[pl.ds(at + u, count, stride=width), :] = split_dot(
                            near, grad, ((1,), (0,))
                        )

                self.when_here(first, (base, width, height), vector if two is None else outer)
            lanes = lax.broadcasted_iota(jnp.int32, (self.packed, LANE), 1)
            index = lax.broadcasted_iota(jnp.int32, (self.packed, LANE), 0)
            back = (LANE - skew) % LANE
            here = pltpu.roll(rows_ref[FRONT : FRONT + self.packed], back, 1)
            after = pltpu.roll(rows_ref[FRONT + 1 : FRONT + 1 + self.packed], back, 1)
            value = jnp.where(lanes < LANE - skew, here, after)
            value = jnp.where(index * LANE + lanes < self.length, value, 0.0)
            grad_ref[...] = value
            square_ref[...] = jnp.sum(
                jnp.sum(value * value, axis=0, keepdims=True), axis=1, keepdims=True
            )

        grad, square = self.call(
            body,
            (
                jax.ShapeDtypeStruct((self.packed, LANE), F32),
                jax.ShapeDtypeStruct((1, 1), F32),
            ),
            operands,
            [pltpu.VMEM((self.total, LANE), F32)],
            name="flat_gradient",
        )
        return grad.reshape(-1)[: self.length], square[0, 0]


def dot(a, b):
    return jnp.dot(a, b, preferred_element_type=F32)


def attend_kernel(block, mixed_ref, bias_ref, out_ref, log_ref, keys, values, query):
    rows = mixed_ref.shape[1]
    wide = mixed_ref[...].astype(F32)
    extra = jnp.concatenate([bias_ref[...], jnp.zeros((7, rows), F32)], axis=0)
    ones = jnp.concatenate([jnp.ones((1, rows), F32), jnp.zeros((7, rows), F32)], axis=0)
    for h in range(HEADS_HERE):
        q = wide[h * HD : (h + 1) * HD]
        k = wide[WIDE + h * HD : WIDE + (h + 1) * HD]
        v = wide[2 * WIDE + h * HD : 2 * WIDE + (h + 1) * HD]
        query[h] = jnp.concatenate([q, ones], axis=0).astype(BF16)
        keys[h] = jnp.concatenate([k, extra], axis=0).T.astype(BF16)
        values[h] = jnp.concatenate([v, jnp.zeros((8, rows), F32)], axis=0).astype(BF16)

    def step(i, unused):
        at = pl.multiple_of(i * block, block)
        outs = []
        logs = []
        for h in range(HEADS_HERE):
            raw = dot(keys[h], query[h, :, pl.ds(at, block)])
            top = jnp.max(raw, axis=0, keepdims=True)
            expo = jnp.exp2((raw - top) * SC2)
            total = jnp.sum(expo, axis=0, keepdims=True)
            out = dot(values[h], expo.astype(BF16))[:HD]
            outs.append(out / total)
            logs.append(top * SC2 + jnp.log2(total))
        out_ref[:, pl.ds(at, block)] = jnp.concatenate(outs, axis=0).astype(BF16)
        log_ref[:, pl.ds(at, block)] = jnp.concatenate(logs + logs, axis=0)
        return unused

    lax.fori_loop(0, rows // block, step, 0)


def attend(mixed, bias, block=512):
    rows = mixed.shape[1]
    return pl.pallas_call(
        functools.partial(attend_kernel, block),
        out_shape=(
            jax.ShapeDtypeStruct((WIDE, rows), BF16),
            jax.ShapeDtypeStruct((8, rows), F32),
        ),
        scratch_shapes=[
            pltpu.VMEM((HEADS_HERE, rows, 80), BF16),
            pltpu.VMEM((HEADS_HERE, 80, rows), BF16),
            pltpu.VMEM((HEADS_HERE, 80, rows), BF16),
        ],
        compiler_params=pltpu.CompilerParams(vmem_limit_bytes=48 * 1024 * 1024),
        cost_estimate=pl.CostEstimate(
            flops=4 * HEADS_HERE * rows * rows * HD,
            bytes_accessed=8 * WIDE * rows,
            transcendentals=HEADS_HERE * rows * rows,
        ),
        name="attend",
    )(mixed, bias)


def attend_back_kernel(
    block, mixed_ref, bias_ref, out_ref, log_ref, grad_ref, result_ref,
    keys, values, query, keys_t, query_t, grads, grads_t, sum_k, sum_v, grad_q, delta,
):
    rows = mixed_ref.shape[1]
    wide = mixed_ref[...].astype(F32)
    gwide = grad_ref[...].astype(F32)
    owide = out_ref[...].astype(F32)
    extra = jnp.concatenate([bias_ref[...], jnp.zeros((7, rows), F32)], axis=0)
    ones = jnp.concatenate([jnp.ones((1, rows), F32), jnp.zeros((7, rows), F32)], axis=0)
    none = jnp.zeros((8, rows), F32)
    deltas = []
    for h in range(HEADS_HERE):
        q = wide[h * HD : (h + 1) * HD]
        k = wide[WIDE + h * HD : WIDE + (h + 1) * HD]
        v = wide[2 * WIDE + h * HD : 2 * WIDE + (h + 1) * HD]
        g = gwide[h * HD : (h + 1) * HD]
        o = owide[h * HD : (h + 1) * HD]
        query[h] = jnp.concatenate([q, ones], axis=0).astype(BF16)
        query_t[h] = jnp.concatenate([q, none], axis=0).T.astype(BF16)
        keys[h] = jnp.concatenate([k, extra], axis=0).T.astype(BF16)
        keys_t[h] = jnp.concatenate([k, none], axis=0).astype(BF16)
        values[h] = jnp.concatenate([v, none], axis=0).T.astype(BF16)
        grads[h] = jnp.concatenate([g, none], axis=0).astype(BF16)
        grads_t[h] = jnp.concatenate([g, none], axis=0).T.astype(BF16)
        deltas.append(jnp.sum(g * o, axis=0, keepdims=True))
    delta[...] = jnp.concatenate(deltas + deltas, axis=0)
    sum_k[...] = jnp.zeros_like(sum_k)
    sum_v[...] = jnp.zeros_like(sum_v)

    def step(i, unused):
        at = pl.multiple_of(i * block, block)
        here = pl.ds(at, block)
        for h in range(HEADS_HERE):
            raw = dot(keys[h], query[h, :, here])
            probs = jnp.exp2(raw * SC2 - log_ref[h : h + 1, here])
            grad_probs = dot(values[h], grads[h, :, here])
            grad_raw = (probs * (grad_probs - delta[h : h + 1, here])).astype(BF16)
            sum_v[h] += dot(probs.astype(BF16), grads_t[h, here, :])
            sum_k[h] += dot(grad_raw, query_t[h, here, :])
            grad_q[h, :, here] = dot(keys_t[h], grad_raw)
        return unused

    lax.fori_loop(0, rows // block, step, 0)
    parts = [grad_q[h][:HD] * SCALE for h in range(HEADS_HERE)]
    parts += [(sum_k[h].T)[:HD] * SCALE for h in range(HEADS_HERE)]
    parts += [(sum_v[h].T)[:HD] for h in range(HEADS_HERE)]
    result_ref[...] = jnp.concatenate(parts, axis=0).astype(BF16)


def attend_back(mixed, bias, out, logs, grad, block=512):
    rows = mixed.shape[1]
    n = HEADS_HERE
    return pl.pallas_call(
        functools.partial(attend_back_kernel, block),
        out_shape=jax.ShapeDtypeStruct((3 * WIDE, rows), BF16),
        scratch_shapes=[
            pltpu.VMEM((n, rows, 80), BF16),
            pltpu.VMEM((n, rows, 80), BF16),
            pltpu.VMEM((n, 80, rows), BF16),
            pltpu.VMEM((n, 80, rows), BF16),
            pltpu.VMEM((n, rows, 80), BF16),
            pltpu.VMEM((n, 80, rows), BF16),
            pltpu.VMEM((n, rows, 80), BF16),
            pltpu.VMEM((n, rows, 80), F32),
            pltpu.VMEM((n, rows, 80), F32),
            pltpu.VMEM((n, 80, rows), F32),
            pltpu.VMEM((8, rows), F32),
        ],
        compiler_params=pltpu.CompilerParams(vmem_limit_bytes=48 * 1024 * 1024),
        cost_estimate=pl.CostEstimate(
            flops=10 * n * rows * rows * HD,
            bytes_accessed=18 * WIDE * rows,
            transcendentals=n * rows * rows,
        ),
        name="attend_back",
    )(mixed, bias, out, logs, grad)


def join_cores(partial):
    low = partial.astype(BF16)
    return low.astype(F32) + lax.ppermute(low, "c", SWAP).astype(F32)


def rank_columns(vector, groups, rank, ranks):
    return lax.dynamic_index_in_dim(
        vector.reshape(groups, ranks, -1), rank, 1, keepdims=False
    ).reshape(-1)


def spread_columns(grads, groups, ranks_here, ranks):
    total = 0.0
    for grad, rank in zip(grads, ranks_here):
        width = grad.shape[0] // groups
        select = (jnp.arange(ranks) == rank).astype(F32)
        total = total + (grad.reshape(groups, 1, width) * select[None, :, None]).reshape(-1)
    return total


class Layer:
    def __init__(self, modulation, biases, ranks_here, ranks, keymask):
        pieces = jnp.split(modulation, 6)
        self.shift_a, self.scale_a, self.gate_a = pieces[:3]
        self.shift_b, self.scale_b, self.gate_b = pieces[3:]
        self.qkv_b, self.proj_b, self.up_b, self.down_b = biases
        self.ranks_here, self.ranks, self.keymask = ranks_here, ranks, keymask

    def take_whole(self, whole, index):
        at = 4 * STRIP * index
        rows = [at, at + STRIP, at + 4 * BLK, at + 8 * BLK, at + 12 * BLK]
        parts = [[whole[i, rows[n] : rows[n + 1]] for i in range(2)] for n in range(4)]
        self.mixer, self.proj, self.up_w, self.down_w = parts

    def take_planes(self, upper, lower):
        self.mixer = [upper[i][0] for i in range(2)]
        self.proj = [upper[i][1][:BLK] for i in range(2)]
        self.up_w = [jnp.concatenate([upper[i][1][BLK:], lower[i][0][: 2 * BLK]]) for i in range(2)]
        self.down_w = [jnp.concatenate([lower[i][0][2 * BLK :], lower[i][1]]) for i in range(2)]

    def mix_one(self, i, normed):
        bias = rank_columns(self.qkv_b, 3, self.ranks_here[i], self.ranks)
        return (contract_cols(self.mixer[i], normed) + bias[:, None]).astype(BF16)

    def mix_first(self, state):
        self.state = state
        normed = modulate(state, self.shift_a, self.scale_a).astype(BF16)
        return normed, self.mix_one(0, normed)

    def mix_second(self, normed, mixed):
        self.normed_a = normed
        out, logs = attend(mixed, self.keymask)
        self.mixed, self.out, self.logs = [mixed], [out], [logs]
        return self.mix_one(1, normed), out

    def attend_rest(self, mixed, out):
        more, logs = attend(mixed, self.keymask)
        self.mixed.append(mixed)
        self.out.append(more)
        self.logs.append(logs)
        return contract_rows(out, self.proj[0]) + contract_rows(more, self.proj[1])

    def join_attend(self, partial):
        self.attn = join_cores(partial) + self.proj_b
        return self.state + self.gate_a * self.attn

    def widen_one(self, i, normed):
        bias = rank_columns(self.up_b, 1, self.ranks_here[i], self.ranks)
        pre = jnp.dot(normed, self.up_w[i], preferred_element_type=F32) + bias
        return pre, gelu_tanh(pre).astype(BF16)

    def widen_first(self, middle):
        self.middle = middle
        normed = modulate(middle, self.shift_b, self.scale_b).astype(BF16)
        return normed, self.widen_one(0, normed)

    def widen_second(self, normed, first):
        self.normed_b = normed
        return first, self.widen_one(1, normed)

    def narrow(self, first, second):
        self.pre = [first[0], second[0]]
        self.act = [first[1], second[1]]
        partial = 0.0
        for mat, one in zip(self.down_w, self.act):
            partial = partial + jnp.dot(one, mat, preferred_element_type=F32)
        self.mlp = join_cores(partial) + self.down_b
        return self.middle + self.gate_b * self.mlp

    def back_narrow(self, grad_out):
        self.grad_out = grad_out
        self.grad_gate_b = jnp.sum(grad_out * self.mlp, axis=0)
        grad_mlp = self.gate_b * grad_out
        self.grad_down_b = jnp.sum(grad_mlp, axis=0)
        grad_mlp = grad_mlp.astype(BF16)
        self.grad_down, grad_pre = ([], [])
        for i in range(2):
            self.grad_down.append(contract_rows(self.act[i], grad_mlp).astype(BF16))
            grad_act = contract_cols(grad_mlp, self.down_w[i])
            unused, gelu_pull = jax.vjp(gelu_tanh, self.pre[i])
            grad_pre.append(gelu_pull(grad_act)[0].astype(BF16))
        return grad_pre

    def back_widen(self, grad_pre, planes, index):
        self.grad_up, self.grad_up_b = ([], [])
        partial = 0.0
        for i in range(2):
            self.grad_up_b.append(jnp.sum(grad_pre[i].astype(F32), axis=0))
            self.grad_up.append(contract_rows(self.normed_b, grad_pre[i]).astype(BF16))
            partial = partial + contract_cols(grad_pre[i], self.up_w[i])
        unused, pull_b = jax.vjp(modulate, self.middle, self.shift_b, self.scale_b)
        grad_inner, self.grad_shift_b, self.grad_scale_b = pull_b(join_cores(partial))
        split = 2 * BLK
        planes[2 * index + 1] = [
            (
                jnp.concatenate([self.grad_up[i][split:], self.grad_down[i][:BLK]]),
                self.grad_down[i][BLK:],
            )
            for i in range(2)
        ]
        return self.grad_out + grad_inner

    def back_one(self, i):
        self.grad_proj.append(
            jnp.dot(self.out[i], self.grad_attn, preferred_element_type=F32).astype(BF16)
        )
        grad_attended = contract_cols(self.proj[i], self.grad_attn).astype(BF16)
        return attend_back(self.mixed[i], self.keymask, self.out[i], self.logs[i], grad_attended)

    def back_attend(self, grad_middle):
        self.grad_middle = grad_middle
        self.grad_gate_a = jnp.sum(grad_middle * self.attn, axis=0)
        grad_attn = self.gate_a * grad_middle
        self.grad_proj_b = jnp.sum(grad_attn, axis=0)
        self.grad_attn = grad_attn.astype(BF16)
        self.grad_proj = []
        return self.back_one(0), self.grad_attn

    def back_rest(self, grad_mixed, grad_attn):
        self.grad_attn = grad_attn
        return grad_mixed, self.back_one(1)

    def back_mix(self, grad_mixed):
        self.grad_mixer, self.grad_qkv_b = ([], [])
        for i in range(2):
            self.grad_qkv_b.append(jnp.sum(grad_mixed[i].astype(F32), axis=1))
            self.grad_mixer.append(
                jnp.dot(grad_mixed[i], self.normed_a, preferred_element_type=F32).astype(BF16)
            )
        return grad_mixed

    def back_join(self, grad_mixed, planes, index):
        grad_mixer, grad_qkv_b = self.grad_mixer, self.grad_qkv_b
        partial = 0.0
        for i in range(2):
            partial = partial + contract_rows(grad_mixed[i], self.mixer[i])
        unused, pull_a = jax.vjp(modulate, self.state, self.shift_a, self.scale_a)
        grad_state, grad_shift_a, grad_scale_a = pull_a(join_cores(partial))
        self.grad_mod = jnp.concatenate(
            [
                grad_shift_a,
                grad_scale_a,
                self.grad_gate_a,
                self.grad_shift_b,
                self.grad_scale_b,
                self.grad_gate_b,
            ]
        )
        once = jnp.where(lax.axis_index("c") == 0, 1.0, 0.0)
        self.grad_bias = jnp.concatenate(
            [
                spread_columns(grad_qkv_b, 3, self.ranks_here, self.ranks),
                self.grad_proj_b * once,
                spread_columns(self.grad_up_b, 1, self.ranks_here, self.ranks),
                self.grad_down_b * once,
            ]
        )
        split = 2 * BLK
        planes[2 * index] = [
            (
                grad_mixer[i],
                jnp.concatenate([self.grad_proj[i], self.grad_up[i][:split]]),
            )
            for i in range(2)
        ]
        return self.grad_middle + grad_state


def adamw(grad, moment, second, master):
    new_moment = ADAM_ONE * moment + (1.0 - ADAM_ONE) * grad
    new_second = ADAM_TWO * second + (1.0 - ADAM_TWO) * grad * grad
    fixed_moment = new_moment / (1.0 - ADAM_ONE**STEP_COUNT)
    fixed_second = new_second / (1.0 - ADAM_TWO**STEP_COUNT)
    new_master = master - ADAM_RATE * (
        fixed_moment / (jnp.sqrt(fixed_second) + ADAM_EPS) + ADAM_DECAY * master
    )
    return (new_moment, new_second, new_master)


def halves_dot(left, right, dims):
    left_high, right_high = left.astype(BF16), right.astype(BF16)
    left_low = (left - left_high.astype(F32)).astype(BF16)
    right_low = (right - right_high.astype(F32)).astype(BF16)

    def product(one, two):
        return lax.dot_general(one, two, (dims, ((), ())), preferred_element_type=F32)

    return product(left_high, right_high) + (
        product(left_high, right_low) + product(left_low, right_high)
    )


def shampoo_kernel(
    factor, grad, moment, left, right, left_inv, right_inv, master, *outs
):
    new_moment, new_left, new_right, new_master = outs
    clipped = grad[...].astype(F32) * factor[0]
    rows, columns = ((1,), (1,)), ((0,), (0,))
    new_left[...] = SHAMPOO_TWO * left[...] + (1.0 - SHAMPOO_TWO) * halves_dot(
        clipped, clipped, rows
    )
    new_right[...] = SHAMPOO_TWO * right[...] + (1.0 - SHAMPOO_TWO) * halves_dot(
        clipped, clipped, columns
    )
    mixed = SHAMPOO_ONE * moment[...] + (1.0 - SHAMPOO_ONE) * clipped
    new_moment[...] = mixed
    halfway = halves_dot(left_inv[...], mixed, ((1,), (0,)))
    direction = halves_dot(halfway, right_inv[...], ((1,), (0,)))
    new_master[...] = master[...] - SHAMPOO_RATE * (direction + SHAMPOO_DECAY * master[...])


def shampoo(factor, grad, moment, left, right, left_inv, right_inv, master):
    block = pl.BlockSpec((None, BLK, BLK), lambda i: (i, 0, 0))
    shape = jax.ShapeDtypeStruct(moment.shape, F32)
    return pl.pallas_call(
        shampoo_kernel,
        grid=(moment.shape[0],),
        out_shape=[shape] * 4,
        in_specs=[pl.BlockSpec(memory_space=pltpu.SMEM)] + [block] * 7,
        out_specs=[block] * 4,
        compiler_params=pltpu.CompilerParams(vmem_limit_bytes=48 * 1024 * 1024),
        name="shampoo",
    )(factor.reshape(1), grad, moment, left, right, left_inv, right_inv, master)


def local(
    latents,
    noise,
    timesteps,
    labels,
    grid,
    flat_master,
    flat_moment,
    flat_second,
    tile_master,
    tile_moment,
    tile_left,
    tile_right,
    left_root,
    right_root,
):
    x, y, z, c = [lax.axis_index(name) for name in ("x", "y", "z", "c")]
    groups = lax.axis_size("z") * lax.axis_size("y")
    ranks = lax.axis_size("x") * lax.axis_size("c")
    count_tiles = tile_master.shape[1]
    simple = lax.axis_size("y") == 2 and lax.axis_size("z") == 4 and count_tiles == 12
    ranks_here = [2 * x + c, 2 * (1 - x) + c]
    number = (z * lax.axis_size("y") + y) * 2 + x

    owner = z * lax.axis_size("y") + y
    is_mixer = owner % 4 == 0
    overlap = Overlap()
    planes = {}
    if simple:
        strip = strips_of(tile_master[0].astype(BF16), is_mixer)[0]
    else:
        gather_any(tile_master[0].astype(BF16), planes)
    flat = Flat(flat_master.shape[0])

    info = jnp.concatenate([timesteps[:, 0], labels[:, 0], grid[:, 0, 0], grid[:, 1, 0]])
    info = gather_rows(info.reshape(1, 4, MB), [("z", "y")])
    info = info.transpose(1, 0, 2).reshape(4, groups * MB)
    patches, target = own_sequence(latents), own_sequence(noise)
    held = flat.align(flat_master)
    overlap.before = [info, patches, target]
    count = jnp.sum((info[2] * info[3]).astype(F32))
    height = lax.dynamic_index_in_dim(info[2], number, 0, keepdims=False)
    width = lax.dynamic_index_in_dim(info[3], number, 0, keepdims=False)
    rows = patches.shape[1]
    slots = jnp.arange(rows)
    valid = slots < height * width
    keymask = jnp.where(valid, 0.0, -1e30).astype(F32)[None]

    freq = jax.vmap(time_freq)(info[0])
    onehot = (jnp.arange(CLASSES)[None, :] == info[1][:, None]).astype(F32)

    stem_axes = (("c",), ("y", "x"), ("z",))
    if BASE_TABLE * LANE <= ranks * flat.length:
        stem_axes = (("x", "c"),)
    w1, w2 = (BASE_W1, ROW_D, FREQ), (BASE_W2, ROW_D, D)
    table = (BASE_TABLE, ROW_D, CLASSES)
    final = (BASE_FINAL, ROW_FINAL, D)
    adas = [(BASE_LAYER + l * LAYER_ROWS, ROW_ADA, D) for l in range(LAYERS)]

    def small_work(held):
        vectors = [(0, ROW_STEM), (BASE_B1, ROW_D), (BASE_B2, ROW_D)]
        vectors += [(BASE_LAYER + l * LAYER_ROWS + D * ROW_ADA, ROW_BIAS) for l in range(LAYERS)]
        small = flat.take(held, vectors + [(BASE_TAIL, ROW_TAIL)]).astype(BF16)
        first = all_sum(small[ROW_STEM : ROW_STEM + ROW_D], stem_axes)
        hidden_pre = all_sum(flat.product(held, [freq], [w1], True, True), stem_axes)
        hidden_pre = hidden_pre + first.astype(F32).reshape(-1)
        hidden = jax.nn.silu(hidden_pre)
        cond = all_sum(
            flat.product(held, [hidden, onehot], [w2, table], True, True), (("c",), ("y", "x"))
        )
        return all_sum(small, (("c",), ("y", "x"))), hidden_pre, hidden, cond, held

    small, hidden_pre, hidden, cond, held = overlap.beside(small_work, held)
    small, cond = overlap.alone(
        lambda *v: [all_sum(one, (("z",),)) for one in v], small, cond
    )
    small = small.astype(F32)
    pieces = []
    at = 0
    for amount in [ROW_STEM, ROW_D, ROW_D] + [ROW_BIAS] * LAYERS + [ROW_TAIL]:
        pieces.append(small[at : at + amount].reshape(-1))
        at = at + amount
    stem, unused, time_b2 = pieces[:3]
    tail = pieces[-1]
    patch_w, patch_b = stem[: PATCH * D].reshape(PATCH, D), stem[PATCH * D :]
    final_b, head_w = tail[: 2 * D], tail[2 * D :].reshape(D, PATCH).astype(BF16)
    biases, ada_bs = ([], [])
    for layer in range(LAYERS):
        vector = pieces[3 + layer]
        ada_bs.append(vector[: 6 * D])
        biases.append(jnp.split(vector[6 * D :], [3 * D, 4 * D, 8 * D]))

    def mod_work(cond, held, small):
        cond = cond + small[ROW_STEM + ROW_D : ROW_STEM + 2 * ROW_D].reshape(-1)
        cond_s = jax.nn.silu(cond).astype(BF16)
        mods = flat.product(held, [cond_s] * 3, adas + [final], False, False)
        return cond, cond_s, columns_by_core(mods)

    cond, cond_s, mods = overlap.beside(mod_work, cond, held, small)
    mods = overlap.alone(lambda v: scatter_rows(v, ("z",)), mods)

    def stem_work(patches, mods):
        mods = columns_of_cores(scatter_rows(mods, ("y", "x")))[0]
        state = contract_rows(patches, patch_w.astype(BF16)) + patch_b + place_embed(slots, width)
        return state, mods

    state, mods = overlap.beside(stem_work, patches, mods)
    if simple:
        strip, state, mods = lax.optimization_barrier((strip, state, mods))
        whole = gather_strips(strip)
        state, whole = lax.optimization_barrier((state, whole))
    final_mod = mods[LAYERS * 6 * D :] + final_b
    layers = [
        Layer(mods[l * 6 * D : (l + 1) * 6 * D] + ada_bs[l], biases[l], ranks_here, ranks, keymask)
        for l in range(LAYERS)
    ]
    for index, layer in enumerate(layers):
        if simple:
            layer.take_whole(whole, index)
        else:
            layer.take_planes(planes[2 * index], planes[2 * index + 1])
        values = overlap.beside(layer.mix_first, state)
        values = overlap.beside(layer.mix_second, *values)
        values = overlap.beside(layer.attend_rest, *values)
        middle = overlap.beside(layer.join_attend, values)
        values = overlap.beside(layer.widen_first, middle)
        values = overlap.beside(layer.widen_second, *values)
        state = overlap.beside(layer.narrow, *values)
    shift_f, scale_f = jnp.split(final_mod, 2)
    normed_f = modulate(state, shift_f, scale_f).astype(BF16)
    predicted = jnp.dot(normed_f, head_w, preferred_element_type=F32)
    error = predicted - target.T
    loss_part = jnp.sum(jnp.where(valid[:, None], error * error, 0.0))
    grad_pred = jnp.where(valid[:, None], 2.0 * error / (PATCH * count), 0.0).astype(BF16)

    grad_head = contract_rows(normed_f, grad_pred)
    grad_normed_f = contract_cols(grad_pred, head_w)
    unused, pull_f = jax.vjp(modulate, state, shift_f, scale_f)
    grad_state, grad_shift_f, grad_scale_f = pull_f(grad_normed_f)
    grad_final = jnp.concatenate([grad_shift_f, grad_scale_f])
    grad_planes = {}
    done = {}
    for index in reversed(range(LAYERS)):
        layer = layers[index]
        grad_pre = overlap.beside(layer.back_narrow, grad_state)
        grad_middle = overlap.beside(
            lambda *v: layer.back_widen(v, grad_planes, index), *grad_pre
        )
        if simple and index == LAYERS - 1:
            overlap.feed(reduce_strips(grad_planes, done))
        grad_mixed = overlap.beside(layer.back_attend, grad_middle)
        grad_mixed = overlap.beside(layer.back_rest, *grad_mixed)
        grad_state = overlap.beside(
            lambda *v: layer.back_join(layer.back_mix(v), grad_planes, index), *grad_mixed
        )

    def factor_work(grad_mods):
        return [gather_rows(one[None], [("y", "x"), ("z",)]) for one in grad_mods]

    mods_of = overlap.alone(factor_work, [layer.grad_mod for layer in layers] + [grad_final])
    mods_of, final_of = mods_of[:LAYERS], mods_of[LAYERS]

    def grad_cond_work(grad_state, mods_of, final_of):
        grad_patch_b = jnp.sum(grad_state, axis=0)
        grad_patch_w = jnp.dot(patches.astype(F32), grad_state, precision=HIGH)
        once = jnp.where(c == 0, 1.0, 0.0)
        summed = jnp.concatenate(
            [grad_patch_w.reshape(-1) * once, grad_patch_b * once]
            + [layer.grad_bias for layer in layers]
            + [grad_head.reshape(-1) * once, jnp.pad(loss_part[None] * once, (0, 2 * LANE - 1))]
        )
        grad_cond = flat.back_product(held, mods_of + [final_of], adas + [final])
        return columns_by_core(summed), grad_cond, mods_of, final_of

    summed, grad_cond, mods_of, final_of = overlap.beside(
        grad_cond_work, grad_state, mods_of, final_of
    )
    grad_cond, mods_of, final_of = overlap.alone(
        lambda v, *more: (all_sum(v),) + more, grad_cond, mods_of, final_of
    )

    def grad_hidden_work(grad_cond, mods_of, final_of):
        grad_cond = jax.vjp(jax.nn.silu, cond)[1](grad_cond)[0]
        return flat.back_product(held, [grad_cond], [w2]), grad_cond, mods_of, final_of

    grad_hidden, grad_cond, mods_of, final_of = overlap.beside(
        grad_hidden_work, grad_cond, mods_of, final_of
    )

    def last_sums(summed, grad_hidden, grad_cond, mods_of, final_of):
        grad_hidden = all_sum(grad_hidden, stem_axes)
        grad_hidden = jax.vjp(jax.nn.silu, hidden_pre)[1](grad_hidden)[0]
        summed = columns_of_cores(all_sum(summed, (("y", "x"), ("z",))))
        return summed.reshape(-1, LANE), grad_hidden, grad_cond, mods_of, final_of

    summed, grad_hidden, grad_cond, mods_of, final_of = overlap.beside(
        last_sums, summed, grad_hidden, grad_cond, mods_of, final_of
    )
    stem_rows = summed[:ROW_STEM]
    extra = ROW_BIAS - ROW_ADA
    bias_rows = [summed[ROW_STEM + l * extra : ROW_STEM + (l + 1) * extra] for l in range(LAYERS)]
    head_rows = summed[ROW_STEM + LAYERS * extra : -2]
    summed_loss = summed[-2, 0]

    def total_rows(values):
        return jnp.sum(values, axis=0).reshape(-1, LANE)

    cond_f = cond_s.astype(F32)

    def flat_work(grad_hidden, grad_cond, mods_of, final_of):
        parts = [
            (0, stem_rows),
            (BASE_W1, ROW_D, freq, grad_hidden),
            (BASE_B1, total_rows(grad_hidden)),
            (BASE_W2, ROW_D, hidden, grad_cond),
            (BASE_B2, total_rows(grad_cond)),
            (BASE_TABLE, ROW_D, onehot, grad_cond),
        ]
        for layer in range(LAYERS):
            base = BASE_LAYER + layer * LAYER_ROWS
            parts.append((base, ROW_ADA, cond_f, mods_of[layer]))
            vector = jnp.concatenate([total_rows(mods_of[layer]), bias_rows[layer]])
            parts.append((base + D * ROW_ADA, vector))
        parts.append((BASE_FINAL, ROW_FINAL, cond_f, final_of))
        parts.append((BASE_TAIL, jnp.concatenate([total_rows(final_of), head_rows])))
        return flat.gradient(parts)

    grad_flat, square_flat = overlap.beside(flat_work, grad_hidden, grad_cond, mods_of, final_of)
    while overlap.source is not None:
        grad_flat, square_flat = overlap.beside(lambda *v: v, grad_flat, square_flat)
    if simple:
        grad_tiles = tiles_of(by_plane(done)[None], is_mixer)
    else:
        grad_tiles = reduce_any(grad_planes, count_tiles)

    square = square_flat + jnp.sum(jnp.square(grad_tiles.astype(F32)))
    norm = jnp.sqrt(all_sum(square.reshape(1, 1))[0, 0])
    factor = jnp.minimum(1.0, CLIP_AT / (norm + 1e-06))
    new_moment, new_second, new_flat = adamw(
        grad_flat * factor, flat_moment, flat_second, flat_master
    )
    tile_mom, new_left, new_right, new_tiles = shampoo(
        factor,
        grad_tiles,
        tile_moment[0],
        tile_left[0],
        tile_right[0],
        left_root[0],
        right_root[0],
        tile_master[0],
    )
    return (
        summed_loss,
        count,
        norm,
        new_moment,
        new_second,
        new_flat,
        tile_mom[None],
        new_left[None],
        new_right[None],
        new_tiles[None],
    )


def solution(mesh):
    deep = 4
    axes = Mesh(
        mesh.devices.reshape(deep, mesh.shape["dp"] // deep, MB, mesh.shape["mp"] // MB),
        ("z", "y", "x", "c"),
    )
    dp, mp, whole = ("z", "y"), ("x", "c"), ("z", "y", "x", "c")
    tile = P(mp, dp, None, None)
    in_specs = (
        P(None, None, whole),
        P(None, None, whole),
        P(None, dp),
        P(None, dp),
        P(None, None, dp),
        P(whole),
        P(whole),
        P(whole),
    ) + (tile,) * 6
    out_specs = (P(), P(), P(), P(whole), P(whole), P(whole)) + (tile,) * 4
    return jax.shard_map(local, mesh=axes, in_specs=in_specs, out_specs=out_specs, check_vma=False)
```
